32 devices in a mesh: section: 4 (over x, core), expert: 4 (over z), dp: 2 (over y).
Axes of the slice: x: 2, y: 2, z: 4, core: 2. Of those that a mesh axis runs over, the one named last changes fastest.
Arguments:
- fwd_in: bfloat16 [4, 384, 2048], P('section', 'expert'), may hold values from -6 to 6
- fwd_routes: int32 [4, 384, 8], P('section', 'expert'), may hold values from 0 to 31, all different within a row; in each aligned block of 96 rows (0 to 95, 96 to 191, ..., all dimensions but the last counted through in order) at most 26 rows name the same one
- fwd_numer: int32 [4, 384, 8], P('section', 'expert'), may hold values from 1 to 255
- bwd_saved: bfloat16 [4, 384, 2048], P('section', 'expert'), may hold values from -6 to 6
- bwd_routes: int32 [4, 384, 8], P('section', 'expert'), may hold values from 0 to 31, all different within a row; in each aligned block of 96 rows (0 to 95, 96 to 191, ..., all dimensions but the last counted through in order) at most 26 rows name the same one
- bwd_numer: int32 [4, 384, 8], P('section', 'expert'), may hold values from 1 to 255
- bwd_grad: bfloat16 [4, 384, 2048], P('section', 'expert'), may hold values from -6 to 6
- w_gate: bfloat16 [4, 32, 2048, 768], P('section', 'expert', None, 'dp'), may hold values from -0.125 to 0.125
- w_up: bfloat16 [4, 32, 2048, 768], P('section', 'expert', None, 'dp'), may hold values from -0.125 to 0.125
- w_down: bfloat16 [4, 32, 768, 2048], P('section', 'expert', 'dp'), may hold values from -0.21875 to 0.21875
Outputs:
- next_fwd: bfloat16 [4, 384, 2048], P('section', 'expert')
- next_bwd: bfloat16 [4, 384, 2048], P('section', 'expert')
- grad_gate: bfloat16 [4, 32, 2048, 768], P('section', 'expert', None, 'dp')
- grad_up: bfloat16 [4, 32, 2048, 768], P('section', 'expert', None, 'dp')
- grad_down: bfloat16 [4, 32, 768, 2048], P('section', 'expert', 'dp')
The draws below stay inside these ranges and needn't reach their ends.
Inputs may be any that keep to these rules, and one draw needn't show every extreme that they name: `fwd_routes`: each token names 8 different experts. In each aligned block of 96 rows (the tokens of one index of expert of one section) no expert is named more than 26 times; in some blocks some expert is named exactly 26 times. `bwd_routes`: each token names 8 different experts. In each aligned block of 96 rows (the tokens of one index of expert of one section) no expert is named more than 26 times; in some blocks some expert is named exactly 26 times.
All inputs are finite; a program needn't handle non-finite values.
Results may differ from the reference program's by a relative error of at most 0.0058.
Values may be sent and summed in bfloat16 or wider, within the bound.
No kernel may reach another device: no remote copies, remote signals or barrier semaphores. Data moves between devices by JAX's collectives and lax.ppermute only.
A program may use at most 192 MiB of HBM per device.

```python
import math
import jax
import jax.numpy as jnp
import numpy as np
from jax import lax

D = 2048
FF = 768
TOP = 8
EXPERTS = 32
TOK_DEV = 96
MOST = 26
TOKENS = 384
N_SECTION = 4


def place_ends(entries, own_key, low, high):
    longest = entries.shape.index(max(entries.shape))
    spots = []
    for shift in (0, 1):
        where = [jax.random.randint(jax.random.fold_in(own_key, axis), (), 0, length) for axis, length in enumerate(entries.shape)]
        where[longest] = (where[longest] + shift) % entries.shape[longest]
        spots.append(tuple(where))
    return entries.at[spots[0]].set(low).at[spots[1]].set(high)


def shard_levels(key, dims, pieces, smallest, largest):
    def one(position, shards_of):
        draws = jax.random.uniform(jax.random.fold_in(jax.random.fold_in(key, 6), position), (shards_of,), jnp.float32, smallest / len(pieces), largest / len(pieces))
        return jnp.repeat(jnp.exp(draws), dims[position] // shards_of).reshape((-1,) + (1,) * (len(dims) - position - 1))

    gain = one(*pieces[0])
    for cut in pieces[1:]:
        gain = gain * one(*cut)
    return gain


def shared_out(stream_key, own, number, rows, number_of, top, limit, slope):
    ranking = jax.random.permutation(stream_key, number_of)
    heavy_load, usual = portions_of(number_of, rows * top, limit, slope, True), portions_of(number_of, rows * top, limit, slope, False)
    places = jnp.arange(number_of)

    def named(sizes, offset_by):
        used = int((sizes > 0).sum())
        fixed = max(1, used // 4)
        moved = fixed + (places - fixed + offset_by * (used - fixed)) % max(1, number_of - fixed)
        return jnp.zeros((number_of,), jnp.int32).at[ranking[jnp.where(places < fixed, places, moved)]].set(jnp.asarray(sizes, jnp.int32))

    sizes = jnp.where(number % 4 == 0, named(heavy_load, number // 4), named(usual, number - number // 4 - 1))
    mixed = jax.random.permutation(jax.random.fold_in(own, 3), number_of)
    giver, sink = mixed[0:number_of // 2 * 2:2], mixed[1:number_of // 2 * 2:2]
    room = jnp.minimum(sizes[giver] - 1, limit - sizes[sink]) // 2
    room = jnp.where((giver == ranking[0]) | (sink == ranking[0]) | (sizes[sink] == 0), 0, jnp.maximum(room, 0))
    moved = jax.random.randint(jax.random.fold_in(own, 4), (number_of // 2,), 0, 1 << 20) % (room + 1)
    sizes = sizes.at[giver].add(-moved).at[sink].add(moved)
    members = jnp.searchsorted(jnp.cumsum(sizes), jnp.arange(rows * top), side="right").astype(jnp.int32)
    grid = members.reshape(top, rows).T
    grid = grid[jax.random.permutation(jax.random.fold_in(own, 1), rows)]
    offset_by = jax.random.randint(jax.random.fold_in(own, 2), (rows, 1), 0, top)
    return jnp.take_along_axis(grid, (jnp.arange(top)[None, :] + offset_by) % top, axis=1)


def portions_of(count, total, bound, slope, full):
    loads = [(1 << 20) // math.isqrt(grade ** slope) + 1 for grade in range(1, count + 1)]
    largest = bound if full else min(bound, max(-(-total // count), total * loads[0] // sum(loads)))
    least = 1 if total - largest >= count - 1 else 0
    given, rest = [largest] + [least] * (count - 1), total - largest - least * (count - 1)
    while rest > 0:
        movable = [i for i in range(1, count) if given[i] < largest] or [i for i in range(1, count) if given[i] < bound]
        whole, left = sum([loads[i] for i in movable]), rest
        for i in movable:
            more = min(bound - given[i], max(1, left * loads[i] // whole), rest)
            given[i] = given[i] + more
            rest = rest - more
    return np.array(given)


def centred(own_key, shape, deviation, reach, shards=(), held_as=jnp.bfloat16):
    loudness = shard_levels(own_key, shape, shards, -0.22, 0.18) if shards else 1.0
    values = jax.random.normal(own_key, shape, jnp.float32) * deviation * loudness
    return jnp.minimum(jnp.maximum(values, -reach), reach).astype(held_as)


def setup_inputs(seed: int = 0) -> dict:
    key_of = jax.random.split(jax.random.key(seed), 11)
    fwd_in = centred(key_of[0], (N_SECTION, TOKENS, D), 1.0, 6.0, ((0, 4), (1, 4)))
    fwd_routes_keys = jax.random.split(jax.random.fold_in(key_of[1], 1), N_SECTION * TOKENS // TOK_DEV)
    fwd_routes_turns = jax.random.permutation(jax.random.fold_in(key_of[1], 3), N_SECTION * TOKENS // TOK_DEV)
    fwd_routes = jax.vmap(lambda own, number: shared_out(jax.random.fold_in(key_of[1], 2), own, number, TOK_DEV, EXPERTS, TOP, MOST, 2))(fwd_routes_keys, fwd_routes_turns).reshape((N_SECTION, TOKENS, TOP))
    fwd_numer = place_ends(jax.random.randint(key_of[2], (N_SECTION, TOKENS, TOP), 1, 256), jax.random.fold_in(key_of[2], 1), 1, 255).astype(jnp.int32)
    bwd_saved = centred(key_of[3], (N_SECTION, TOKENS, D), 1.0, 6.0, ((0, 4), (1, 4)))
    bwd_routes_keys = jax.random.split(jax.random.fold_in(key_of[4], 1), N_SECTION * TOKENS // TOK_DEV)
    bwd_routes_turns = jax.random.permutation(jax.random.fold_in(key_of[4], 3), N_SECTION * TOKENS // TOK_DEV)
    bwd_routes = jax.vmap(lambda own, number: shared_out(jax.random.fold_in(key_of[4], 2), own, number, TOK_DEV, EXPERTS, TOP, MOST, 2))(bwd_routes_keys, bwd_routes_turns).reshape((N_SECTION, TOKENS, TOP))
    bwd_numer = place_ends(jax.random.randint(key_of[5], (N_SECTION, TOKENS, TOP), 1, 256), jax.random.fold_in(key_of[5], 1), 1, 255).astype(jnp.int32)
    bwd_grad = centred(key_of[6], (N_SECTION, TOKENS, D), 1.0, 6.0, ((0, 4), (1, 4)))
    w_gate = centred(key_of[7], (N_SECTION, EXPERTS, D, FF), D ** -0.5, 0.125, ((0, 4), (1, 4), (3, 2)))
    w_up = centred(key_of[8], (N_SECTION, EXPERTS, D, FF), D ** -0.5, 0.125, ((0, 4), (1, 4), (3, 2)))
    w_down = centred(key_of[9], (N_SECTION, EXPERTS, FF, D), FF ** -0.5, 0.21875, ((0, 4), (1, 4), (2, 2)))
    return {"fwd_in": fwd_in, "fwd_routes": fwd_routes, "fwd_numer": fwd_numer, "bwd_saved": bwd_saved, "bwd_routes": bwd_routes, "bwd_numer": bwd_numer, "bwd_grad": bwd_grad, "w_gate": w_gate, "w_up": w_up, "w_down": w_down}


def slot_positions(routes, capacity):
    flat_routes = routes.reshape(-1)
    onehot_table = (flat_routes[:, None] == jnp.arange(EXPERTS, dtype=jnp.int32)[None, :]).astype(jnp.int32)
    earlier = jnp.cumsum(onehot_table, 0) - onehot_table
    return (flat_routes * capacity + jnp.sum(earlier * onehot_table, 1)).astype(jnp.int32)


def combine_weights(numerators):
    counted = numerators.astype(jnp.float32)
    return counted / jnp.sum(counted, -1, keepdims=True)


def expert_buffer(rows, positions, capacity):
    filled = jnp.zeros((EXPERTS * capacity, rows.shape[-1]), rows.dtype).at[positions].set(rows)
    return filled.reshape(EXPERTS, capacity, rows.shape[-1])


def forward_expert(operands):
    rows, gate_weight, up_weight, down_weight = operands
    gate_value = jnp.dot(rows, gate_weight, preferred_element_type=jnp.float32)
    up_value = jnp.dot(rows, up_weight, preferred_element_type=jnp.float32)
    hidden = (jax.nn.silu(gate_value) * up_value).astype(jnp.bfloat16)
    return jnp.dot(hidden, down_weight, preferred_element_type=jnp.float32).astype(jnp.bfloat16)


def backward_expert(operands):
    rows, grad_rows, gate_weight, up_weight, down_weight = operands
    gate_value = jnp.dot(rows, gate_weight, preferred_element_type=jnp.float32)
    up_value = jnp.dot(rows, up_weight, preferred_element_type=jnp.float32)
    silu_gate = jax.nn.silu(gate_value)
    sigmoid_gate = jax.nn.sigmoid(gate_value)
    hidden = (silu_gate * up_value).astype(jnp.bfloat16)
    hidden_grad = jnp.dot(grad_rows, down_weight.T, preferred_element_type=jnp.float32)
    up_grad = (hidden_grad * silu_gate).astype(jnp.bfloat16)
    gate_grad = (hidden_grad * up_value * sigmoid_gate * (1.0 + gate_value * (1.0 - sigmoid_gate))).astype(jnp.bfloat16)
    row_grad = (jnp.dot(gate_grad, gate_weight.T, preferred_element_type=jnp.float32)
                + jnp.dot(up_grad, up_weight.T, preferred_element_type=jnp.float32)).astype(jnp.bfloat16)
    down_sum = jnp.dot(hidden.T, grad_rows, preferred_element_type=jnp.float32).astype(jnp.bfloat16)
    gate_sum = jnp.dot(rows.T, gate_grad, preferred_element_type=jnp.float32).astype(jnp.bfloat16)
    up_sum = jnp.dot(rows.T, up_grad, preferred_element_type=jnp.float32).astype(jnp.bfloat16)
    return row_grad, gate_sum, up_sum, down_sum


def reference(fwd_in, fwd_routes, fwd_numer, bwd_saved, bwd_routes, bwd_numer, bwd_grad, w_gate, w_up, w_down):
    capacity = TOKENS // TOK_DEV * MOST
    outputs_list = []
    inputs_grads = []
    gate_grads = []
    up_grads = []
    down_grads = []
    for section_idx in range(N_SECTION):
        inputs = fwd_in[section_idx]
        positions = slot_positions(fwd_routes[section_idx], capacity)
        rows = expert_buffer(jnp.repeat(inputs, TOP, 0), positions, capacity)
        expert_out = lax.map(forward_expert, (rows, w_gate[section_idx], w_up[section_idx], w_down[section_idx]))
        picked = expert_out.reshape(-1, D)[positions].reshape(TOKENS, TOP, D).astype(jnp.float32)
        mixing = combine_weights(fwd_numer[section_idx])
        layer_out = (inputs.astype(jnp.float32) + jnp.sum(mixing[:, :, None] * picked, 1)).astype(jnp.bfloat16)
        outputs_list.append(layer_out)

        saved = bwd_saved[section_idx]
        grad_in = bwd_grad[section_idx]
        back_positions = slot_positions(bwd_routes[section_idx], capacity)
        back_mixing = combine_weights(bwd_numer[section_idx])
        scaled_grad = (back_mixing[:, :, None] * grad_in.astype(jnp.float32)[:, None, :]).astype(jnp.bfloat16)
        saved_rows = expert_buffer(jnp.repeat(saved, TOP, 0), back_positions, capacity)
        grad_rows = expert_buffer(scaled_grad.reshape(-1, D), back_positions, capacity)
        row_grad, gate_sum, up_sum, down_sum = lax.map(
            backward_expert, (saved_rows, grad_rows, w_gate[section_idx], w_up[section_idx], w_down[section_idx]))
        picked_grad = row_grad.reshape(-1, D)[back_positions].reshape(TOKENS, TOP, D).astype(jnp.float32)
        input_grad = (grad_in.astype(jnp.float32) + jnp.sum(picked_grad, 1)).astype(jnp.bfloat16)
        inputs_grads.append(input_grad)
        gate_grads.append(gate_sum)
        up_grads.append(up_sum)
        down_grads.append(down_sum)
    next_fwd = jnp.roll(jnp.stack(outputs_list), 1, 0)
    next_bwd = jnp.roll(jnp.stack(inputs_grads), -1, 0)
    return next_fwd, next_bwd, jnp.stack(gate_grads), jnp.stack(up_grads), jnp.stack(down_grads)
```

```python
import functools

import jax
import jax.numpy as jnp
from jax import lax
from jax.experimental import pallas as pl
from jax.experimental.pallas import tpu as pltpu
from jax.sharding import PartitionSpec as P

EXPERTS = 32
MOST = 26
ROTATED = 8
BF16 = jnp.bfloat16
F32 = jnp.float32
MIB = 1 << 20

NN = (((1,), (0,)), ((), ()))
NT = (((1,), (1,)), ((), ()))
TN = (((0,), (0,)), ((), ()))


def dot(a, b, dims=NN):
    return lax.dot_general(a, b, dims, preferred_element_type=F32)


def rotate(block, axis, distance):
    n = lax.axis_size(axis)
    return lax.ppermute(block, axis, [(i, (i + distance) % n) for i in range(n)])


def params(mib=40):
    return pltpu.CompilerParams(vmem_limit_bytes=mib * MIB)


def cost(flops, nbytes):
    return pl.CostEstimate(flops=int(flops), bytes_accessed=int(nbytes), transcendentals=0)


def fill_onehot(dest_ref, onehot_ref, slots):
    local, tokens = dest_ref.shape
    place = lax.broadcasted_iota(jnp.int32, (slots, tokens), 0)
    for l in range(local):
        onehot_ref[l * slots : (l + 1) * slots, :] = (
            jnp.where(place == dest_ref[l : l + 1, :], 1.0, 0.0).astype(BF16)
        )


def stack_pieces(pieces, rows_ref):
    at = 0
    for piece in pieces:
        rows_ref[at : at + piece.shape[0], :] = piece[...]
        at += piece.shape[0]


def order_kernel(n_pieces, n_arrays, slots, *refs):
    dest_ref, weight_ref = refs[:2]
    pieces = refs[2 : 2 + n_pieces * n_arrays]
    outs = refs[2 + n_pieces * n_arrays : 2 + n_pieces * n_arrays + n_arrays]
    onehot_ref, rows_ref, slot_weight_ref = refs[2 + n_pieces * n_arrays + n_arrays :]
    local, tokens = dest_ref.shape

    @pl.when(pl.program_id(0) == 0)
    def _():
        fill_onehot(dest_ref, onehot_ref, slots)
        if n_arrays > 1:
            for l in range(local):
                part = slice(l * slots, (l + 1) * slots)
                slot_weight_ref[part, :] = jnp.sum(
                    onehot_ref[part, :].astype(F32) * weight_ref[l : l + 1, :], 1, keepdims=True
                )

    for a in range(n_arrays):
        stack_pieces(pieces[a * n_pieces : (a + 1) * n_pieces], rows_ref)
        ordered = dot(onehot_ref[...], rows_ref[...])
        if a == 1:
            ordered = ordered * slot_weight_ref[...]
        outs[a][...] = ordered.astype(BF16)


def in_expert_order(dest, weight, arrays, slots):
    local, tokens = dest.shape
    width = arrays[0][0].shape[1]
    chunk = min(512, width)
    n_pieces, n_arrays = len(arrays[0]), len(arrays)
    whole = pl.BlockSpec((local, tokens), lambda c: (0, 0))
    flat = [piece for pieces in arrays for piece in pieces]
    total = local * slots
    return pl.pallas_call(
        functools.partial(order_kernel, n_pieces, n_arrays, slots),
        grid=(width // chunk,),
        in_specs=[whole, whole]
        + [pl.BlockSpec((piece.shape[0], chunk), lambda c: (0, c)) for piece in flat],
        out_specs=[pl.BlockSpec((total, chunk), lambda c: (0, c))] * n_arrays,
        out_shape=[jax.ShapeDtypeStruct((total, width), BF16)] * n_arrays,
        scratch_shapes=[
            pltpu.VMEM((total, tokens), BF16),
            pltpu.VMEM((tokens, chunk), BF16),
            pltpu.VMEM((total, 1), F32),
        ],
        compiler_params=params(),
        cost_estimate=cost(
            2 * total * tokens * width * n_arrays, 2 * (total + tokens) * width * n_arrays
        ),
        name="order_rows",
    )(dest, weight, *flat)


def combine_kernel(weighted, slots, dest_ref, weight_ref, rows_ref, keep_ref, send_ref, mix_ref):
    tokens, local = dest_ref.shape
    total = rows_ref.shape[0]

    @pl.when(pl.program_id(0) == 0)
    def _():
        slot = lax.broadcasted_iota(jnp.int32, (tokens, total), 1)
        mix = jnp.zeros((tokens, total), F32)
        for l in range(local):
            here = dest_ref[:, l : l + 1]
            here = jnp.where(here >= 0, here + l * slots, -1)
            value = weight_ref[:, l : l + 1] if weighted else 1.0
            mix = jnp.where(slot == here, value, mix)
        mix_ref[...] = mix.astype(BF16)

    half = tokens // 2
    summed = dot(mix_ref[...], rows_ref[...]).astype(BF16)
    keep_ref[...] = summed[:half]
    send_ref[...] = summed[half:]


def token_sums(dest, weight, rows, slots, weighted, part, parts):
    tokens, local = dest.shape
    total, width = rows.shape
    width = width // parts
    chunk = min(512, width)
    steps = width // chunk
    whole = pl.BlockSpec((tokens, local), lambda c: (0, 0))
    return pl.pallas_call(
        functools.partial(combine_kernel, weighted, slots),
        grid=(steps,),
        in_specs=[
            whole,
            whole,
            pl.BlockSpec((total, chunk), lambda c: (0, c + part * steps)),
        ],
        out_specs=[pl.BlockSpec((tokens // 2, chunk), lambda c: (0, c))] * 2,
        out_shape=[jax.ShapeDtypeStruct((tokens // 2, width), BF16)] * 2,
        scratch_shapes=[pltpu.VMEM((tokens, total), BF16)],
        compiler_params=params(),
        cost_estimate=cost(2 * total * tokens * width, 2 * (total + tokens) * width),
        name="token_sums",
    )(dest, weight, rows)


def forward_kernel(rows_ref, gate_ref, up_ref, down_ref, out_ref):
    rows = rows_ref[...]
    gate_value = dot(rows, gate_ref[0])
    up_value = dot(rows, up_ref[0])
    hidden = (gate_value / (1.0 + jnp.exp(-gate_value)) * up_value).astype(BF16)
    out_ref[...] = dot(hidden, down_ref[0]).astype(BF16)


def backward_kernel(
    rows_ref, grad_ref, gate_ref, up_ref, down_ref, hidden_ref, gate_grad_ref, up_grad_ref, out_ref
):
    rows = rows_ref[...]
    gate_value = dot(rows, gate_ref[0])
    up_value = dot(rows, up_ref[0])
    hidden_grad = dot(grad_ref[...], down_ref[0], NT)
    sig = 1.0 / (1.0 + jnp.exp(-gate_value))
    silu = gate_value * sig
    hidden_ref[...] = (silu * up_value).astype(BF16)
    up_grad = (hidden_grad * silu).astype(BF16)
    gate_grad = (hidden_grad * up_value * sig * (1.0 + gate_value * (1.0 - sig))).astype(BF16)
    up_grad_ref[...] = up_grad
    gate_grad_ref[...] = gate_grad
    out_ref[...] = (dot(gate_grad, gate_ref[0], NT) + dot(up_grad, up_ref[0], NT)).astype(BF16)


def weights_kernel(
    rows_ref, grad_ref, hidden_ref, gate_grad_ref, up_grad_ref, gate_ref, up_ref, down_ref
):
    rows = rows_ref[...]
    gate_ref[0] = dot(rows, gate_grad_ref[...], TN).astype(BF16)
    up_ref[0] = dot(rows, up_grad_ref[...], TN).astype(BF16)
    down_ref[0] = dot(hidden_ref[...], grad_ref[...], TN).astype(BF16)


def expert_specs(local, slots, width, hidden):
    wide = pl.BlockSpec((slots, width), lambda e: (e, 0))
    narrow = pl.BlockSpec((slots, hidden), lambda e: (e, 0))
    column = pl.BlockSpec((1, width, hidden), lambda e: (e, 0, 0))
    row = pl.BlockSpec((1, hidden, width), lambda e: (e, 0, 0))
    return wide, narrow, column, row


def forward_experts(rows, gate, up, down):
    local, width, hidden = gate.shape
    slots = rows.shape[0] // local
    wide, narrow, column, row = expert_specs(local, slots, width, hidden)
    return pl.pallas_call(
        forward_kernel,
        grid=(local,),
        in_specs=[wide, column, column, row],
        out_specs=wide,
        out_shape=jax.ShapeDtypeStruct(rows.shape, BF16),
        compiler_params=params(),
        cost_estimate=cost(6 * rows.shape[0] * width * hidden, 6 * local * width * hidden),
        name="forward_experts",
    )(rows, gate, up, down)


def backward_experts(rows, grads, gate, up, down):
    local, width, hidden = gate.shape
    slots = rows.shape[0] // local
    wide, narrow, column, row = expert_specs(local, slots, width, hidden)
    small = jax.ShapeDtypeStruct((rows.shape[0], hidden), BF16)
    return pl.pallas_call(
        backward_kernel,
        grid=(local,),
        in_specs=[wide, wide, column, column, row],
        out_specs=[narrow, narrow, narrow, wide],
        out_shape=[small, small, small, jax.ShapeDtypeStruct(rows.shape, BF16)],
        compiler_params=params(),
        cost_estimate=cost(10 * rows.shape[0] * width * hidden, 6 * local * width * hidden),
        name="backward_experts",
    )(rows, grads, gate, up, down)


def weight_grads(rows, grads, hidden_rows, gate_grad, up_grad, local):
    width, hidden = rows.shape[1], gate_grad.shape[1]
    slots = rows.shape[0] // local
    wide, narrow, column, row = expert_specs(local, slots, width, hidden)
    return pl.pallas_call(
        weights_kernel,
        grid=(local,),
        in_specs=[wide, wide, narrow, narrow, narrow],
        out_specs=[column, column, row],
        out_shape=[
            jax.ShapeDtypeStruct((local, width, hidden), BF16),
            jax.ShapeDtypeStruct((local, width, hidden), BF16),
            jax.ShapeDtypeStruct((local, hidden, width), BF16),
        ],
        compiler_params=params(),
        cost_estimate=cost(6 * rows.shape[0] * width * hidden, 6 * local * width * hidden),
        name="weight_grads",
    )(rows, grads, hidden_rows, gate_grad, up_grad)


def halves(block, dp_index):
    half = block.shape[0] // 2
    mine = lax.dynamic_slice_in_dim(block, dp_index * half, half, 0)
    other = lax.dynamic_slice_in_dim(block, (1 - dp_index) * half, half, 0)
    return mine, other


def spread(mine, other, groups):
    if groups > ROTATED:
        near = lax.all_gather(mine, "expert", tiled=True)
        return [near, rotate(near, "dp", 1)]
    near = [rotate(mine, "expert", r) for r in range(1, groups)]
    far = [rotate(piece, "dp", 1) for piece in near]
    return [mine] + near + [other] + far


def spread_meta(meta, dp_index, groups):
    half = meta.shape[0] // 2
    both = jnp.concatenate(halves(meta, dp_index), 0)
    if groups > ROTATED:
        metas = list(lax.all_gather(both, "expert"))
    else:
        metas = [both] + [rotate(both, "expert", r) for r in range(1, groups)]
    return jnp.concatenate([m[:half] for m in metas] + [m[half:] for m in metas], 0)


def sums_home(keep, send, groups):
    half = keep.shape[0] // groups
    pair = (keep.astype(F32) + rotate(send, "dp", 1).astype(F32)).astype(BF16)
    pair = pair.reshape(groups, half, -1)
    if groups > ROTATED:
        return jnp.sum(lax.all_to_all(pair, "expert", 0, 0, tiled=True).astype(F32), 0)
    total = pair[0].astype(F32)
    for r in range(1, groups):
        total = total + rotate(pair[r], "expert", -r).astype(F32)
    return total


def to_section(mine, direction, dp_index):
    n, m = lax.axis_size("section"), lax.axis_size("dp")
    same = rotate(mine, "section", direction)
    route = [
        (s * m + d, ((s + direction) % n) * m + (m - 1 - d)) for s in range(n) for d in range(m)
    ]
    cross = lax.ppermute(mine, ("section", "dp"), route)
    first = jnp.where(dp_index == 0, same, cross)
    second = jnp.where(dp_index == 0, cross, same)
    return jnp.concatenate([first, second], 0)


def slot_tables(meta, choices, base, local):
    tokens = meta.shape[0]
    meta = meta.reshape(tokens, 2, 2, choices)
    routes, counted = meta[:, :, 0], meta[:, :, 1].astype(F32)
    mixing = counted / jnp.sum(counted, -1, keepdims=True)
    hit = (routes[..., None] - base) == jnp.arange(local, dtype=jnp.int32)
    weight = jnp.sum(jnp.where(hit, mixing[..., None], 0.0), 2)
    chosen = jnp.any(hit, 2).astype(jnp.int32)
    rank = jnp.cumsum(chosen, 0) - chosen
    return jnp.where(chosen > 0, rank, -1), weight


def local(
    fwd_in, fwd_routes, fwd_numer, bwd_saved, bwd_routes, bwd_numer, bwd_grad, w_gate, w_up, w_down
):
    groups = lax.axis_size("expert")
    group, dp_index = lax.axis_index("expert"), lax.axis_index("dp")
    gate, up, down = w_gate[0], w_up[0], w_down[0]
    n_local = gate.shape[0]
    choices = fwd_routes.shape[-1]
    slots = -(-groups * MOST // 16) * 16

    meta = jnp.concatenate([fwd_routes[0], fwd_numer[0], bwd_routes[0], bwd_numer[0]], -1)
    meta_all = spread_meta(meta, dp_index, groups)
    dest, weight = slot_tables(meta_all, choices, group * n_local, n_local)
    fwd_dest, back_dest = dest[:, 0], dest[:, 1]
    fwd_weight, back_weight = weight[:, 0], weight[:, 1]

    saved_mine, saved_other = halves(bwd_saved[0], dp_index)
    grad_mine, grad_other = halves(bwd_grad[0], dp_index)
    in_mine, in_other = halves(fwd_in[0], dp_index)
    saved = spread(saved_mine, saved_other, groups)
    grads = spread(grad_mine, grad_other, groups)
    inputs = spread(in_mine, in_other, groups)

    saved_rows, grad_rows = in_expert_order(back_dest.T, back_weight.T, [saved, grads], slots)
    hidden, gate_grad, up_grad, row_grad = backward_experts(saved_rows, grad_rows, gate, up, down)
    (in_rows,) = in_expert_order(fwd_dest.T, fwd_weight.T, [inputs], slots)
    out_rows = forward_experts(in_rows, gate, up, down)

    parts = 2

    def returned(dest, weight, rows, weighted):
        return jnp.concatenate(
            [
                sums_home(*token_sums(dest, weight, rows, slots, weighted, part, parts), groups)
                for part in range(parts)
            ],
            1,
        )

    back_sum = returned(back_dest, back_weight, row_grad, False)
    out_sum = returned(fwd_dest, fwd_weight, out_rows, True)
    input_grad = (grad_mine.astype(F32) + back_sum).astype(BF16)
    layer_out = (in_mine.astype(F32) + out_sum).astype(BF16)
    next_bwd = to_section(input_grad, -1, dp_index)
    next_fwd = to_section(layer_out, 1, dp_index)

    gate_sum, up_sum, down_sum = weight_grads(
        saved_rows, grad_rows, hidden, gate_grad, up_grad, n_local
    )
    return (next_fwd[None], next_bwd[None], gate_sum[None], up_sum[None], down_sum[None])


def solution(mesh):
    in_specs = (
        P("section", "expert", None),
        P("section", "expert", None),
        P("section", "expert", None),
        P("section", "expert", None),
        P("section", "expert", None),
        P("section", "expert", None),
        P("section", "expert", None),
        P("section", "expert", None, "dp"),
        P("section", "expert", None, "dp"),
        P("section", "expert", "dp", None),
    )
    out_specs = (
        P("section", "expert", None),
        P("section", "expert", None),
        P("section", "expert", None, "dp"),
        P("section", "expert", None, "dp"),
        P("section", "expert", "dp", None),
    )
    return jax.shard_map(local, mesh=mesh, in_specs=in_specs, out_specs=out_specs, check_vma=False)
```

```python
import functools

import jax
import jax.numpy as jnp
from jax import lax
from jax.experimental import pallas as pl
from jax.experimental.pallas import tpu as pltpu
from jax.sharding import PartitionSpec as P

EXPERTS = 32
MOST = 26
BF16 = jnp.bfloat16
F32 = jnp.float32
MIB = 1 << 20

NN = (((1,), (0,)), ((), ()))
NT = (((1,), (1,)), ((), ()))
TN = (((0,), (0,)), ((), ()))


def dot(a, b, dims=NN):
    return lax.dot_general(a, b, dims, preferred_element_type=F32)


def rotate(block, axis, distance):
    n = lax.axis_size(axis)
    return lax.ppermute(block, axis, [(i, (i + distance) % n) for i in range(n)])


def swap(block, axis, mask):
    n = lax.axis_size(axis)
    return lax.ppermute(block, axis, [(i, i ^ mask) for i in range(n)])


def after(value, *others):
    return lax.optimization_barrier((value, *others))[0]


def params(mib=40):
    return pltpu.CompilerParams(vmem_limit_bytes=mib * MIB)


def cost(flops, nbytes):
    return pl.CostEstimate(flops=int(flops), bytes_accessed=int(nbytes), transcendentals=0)


def routing_kernel(slots, dest_ref, weight_ref, dest_col_ref, weight_col_ref, *refs):
    ordered_refs, mix_refs, slot_weight_ref = refs[:2], refs[2:4], refs[4]
    total, tokens = ordered_refs[0].shape
    local = total // slots
    place = lax.broadcasted_iota(jnp.int32, (slots, tokens), 0)
    slot = lax.broadcasted_iota(jnp.int32, (tokens, total), 1)
    for way in range(2):
        mix = jnp.zeros((tokens, total), F32)
        for l in range(local):
            at = way * local + l
            part = slice(l * slots, (l + 1) * slots)
            hit = place == dest_ref[at : at + 1, :]
            ordered_refs[way][part, :] = jnp.where(hit, 1.0, 0.0).astype(BF16)
            if way == 1:
                slot_weight_ref[part, :] = jnp.sum(
                    jnp.where(hit, weight_ref[at : at + 1, :], 0.0), 1, keepdims=True
                )
            here = dest_col_ref[:, at : at + 1]
            here = jnp.where(here >= 0, here + l * slots, -1)
            value = weight_col_ref[:, at : at + 1] if way == 0 else 1.0
            mix = jnp.where(slot == here, value, mix)
        mix_refs[way][...] = mix.astype(BF16)


def routing_matrices(dest, weight, slots):
    tokens, both = dest.shape
    total = both // 2 * slots
    return pl.pallas_call(
        functools.partial(routing_kernel, slots),
        out_shape=[jax.ShapeDtypeStruct((total, tokens), BF16)] * 2
        + [jax.ShapeDtypeStruct((tokens, total), BF16)] * 2
        + [jax.ShapeDtypeStruct((total, 1), F32)],
        compiler_params=params(48),
        cost_estimate=cost(0, 8 * total * tokens),
        name="routing",
    )(dest.T, weight.T, dest, weight)


def order_kernel(n_pieces, onehot_ref, *refs):
    *pieces, out_ref, rows_ref = refs
    at = 0
    for piece in pieces:
        rows_ref[at : at + piece.shape[0], :] = piece[...]
        at += piece.shape[0]
    out_ref[...] = dot(onehot_ref[...], rows_ref[...]).astype(BF16)


def weighted_order_kernel(n_pieces, plain, onehot_ref, slot_weight_ref, *refs):
    *pieces, out_ref, rows_ref = refs
    at = 0
    for piece in pieces:
        rows_ref[at : at + piece.shape[0], :] = piece[...]
        at += piece.shape[0]
    ordered = dot(onehot_ref[...], rows_ref[...])
    scale = jnp.where(pl.program_id(0) < plain, 1.0, slot_weight_ref[...])
    out_ref[...] = (ordered * scale).astype(BF16)


def in_expert_order(onehot, pieces, slot_weight=None):
    total, tokens = onehot.shape
    width = pieces[0].shape[1]
    chunk = min(512, width)
    steps = width // chunk
    in_specs = [pl.BlockSpec((total, tokens), lambda c: (0, 0))]
    operands = [onehot]
    if slot_weight is None:
        kernel = functools.partial(order_kernel, len(pieces))
    else:
        kernel = functools.partial(weighted_order_kernel, len(pieces), steps // 2)
        in_specs.append(pl.BlockSpec((total, 1), lambda c: (0, 0)))
        operands.append(slot_weight)
    in_specs += [pl.BlockSpec((piece.shape[0], chunk), lambda c: (0, c)) for piece in pieces]
    return pl.pallas_call(
        kernel,
        grid=(steps,),
        in_specs=in_specs,
        out_specs=pl.BlockSpec((total, chunk), lambda c: (0, c)),
        out_shape=jax.ShapeDtypeStruct((total, width), BF16),
        scratch_shapes=[pltpu.VMEM((tokens, chunk), BF16)],
        compiler_params=params(),
        cost_estimate=cost(2 * total * tokens * width, 2 * (total + tokens) * width),
        name="order_rows",
    )(*operands, *pieces)


def combine_kernel(mix_ref, rows_ref, keep_ref, send_ref):
    half = mix_ref.shape[0] // 2
    summed = dot(mix_ref[...], rows_ref[...]).astype(BF16)
    keep_ref[...] = summed[:half]
    send_ref[...] = summed[half:]


def token_sums(mix, rows, part, parts):
    tokens, total = mix.shape
    width = rows.shape[1] // parts
    chunk = min(512, width)
    steps = width // chunk
    return pl.pallas_call(
        combine_kernel,
        grid=(steps,),
        in_specs=[
            pl.BlockSpec((tokens, total), lambda c: (0, 0)),
            pl.BlockSpec((total, chunk), lambda c: (0, c + part * steps)),
        ],
        out_specs=[pl.BlockSpec((tokens // 2, chunk), lambda c: (0, c))] * 2,
        out_shape=[jax.ShapeDtypeStruct((tokens // 2, width), BF16)] * 2,
        compiler_params=params(),
        cost_estimate=cost(2 * total * tokens * width, 2 * (total + tokens) * width),
        name="token_sums",
    )(mix, rows)


def forward_kernel(rows_ref, gate_ref, up_ref, down_ref, out_ref):
    rows = rows_ref[...]
    gate_value = dot(rows, gate_ref[0])
    up_value = dot(rows, up_ref[0])
    hidden = (gate_value / (1.0 + jnp.exp(-gate_value)) * up_value).astype(BF16)
    out_ref[...] = dot(hidden, down_ref[0]).astype(BF16)


def backward_kernel(
    rows_ref, grad_ref, gate_ref, up_ref, down_ref, hidden_ref, gate_grad_ref, up_grad_ref, out_ref
):
    rows = rows_ref[...]
    gate_value = dot(rows, gate_ref[0])
    up_value = dot(rows, up_ref[0])
    hidden_grad = dot(grad_ref[...], down_ref[0], NT)
    sig = 1.0 / (1.0 + jnp.exp(-gate_value))
    silu = gate_value * sig
    hidden_ref[...] = (silu * up_value).astype(BF16)
    up_grad = (hidden_grad * silu).astype(BF16)
    gate_grad = (hidden_grad * up_value * sig * (1.0 + gate_value * (1.0 - sig))).astype(BF16)
    up_grad_ref[...] = up_grad
    gate_grad_ref[...] = gate_grad
    out_ref[...] = (dot(gate_grad, gate_ref[0], NT) + dot(up_grad, up_ref[0], NT)).astype(BF16)


def weights_kernel(
    rows_ref, grad_ref, hidden_ref, gate_grad_ref, up_grad_ref, gate_ref, up_ref, down_ref
):
    rows = rows_ref[...]
    gate_ref[0] = dot(rows, gate_grad_ref[...], TN).astype(BF16)
    up_ref[0] = dot(rows, up_grad_ref[...], TN).astype(BF16)
    down_ref[0] = dot(hidden_ref[...], grad_ref[...], TN).astype(BF16)


def expert_specs(local, slots, width, hidden):
    wide = pl.BlockSpec((slots, width), lambda e: (e, 0))
    narrow = pl.BlockSpec((slots, hidden), lambda e: (e, 0))
    column = pl.BlockSpec((1, width, hidden), lambda e: (e, 0, 0))
    row = pl.BlockSpec((1, hidden, width), lambda e: (e, 0, 0))
    return wide, narrow, column, row


def forward_experts(rows, gate, up, down):
    local, width, hidden = gate.shape
    slots = rows.shape[0] // local
    wide, narrow, column, row = expert_specs(local, slots, width, hidden)
    return pl.pallas_call(
        forward_kernel,
        grid=(local,),
        in_specs=[wide, column, column, row],
        out_specs=wide,
        out_shape=jax.ShapeDtypeStruct(rows.shape, BF16),
        compiler_params=params(),
        cost_estimate=cost(6 * rows.shape[0] * width * hidden, 6 * local * width * hidden),
        name="forward_experts",
    )(rows, gate, up, down)


def backward_experts(both, gate, up, down):
    local, width, hidden = gate.shape
    total = both.shape[0]
    slots = total // local
    wide, narrow, column, row = expert_specs(local, slots, width, hidden)
    grad_wide = pl.BlockSpec((slots, width), lambda e: (e, 1))
    small = jax.ShapeDtypeStruct((total, hidden), BF16)
    return pl.pallas_call(
        backward_kernel,
        grid=(local,),
        in_specs=[wide, grad_wide, column, column, row],
        out_specs=[narrow, narrow, narrow, wide],
        out_shape=[small, small, small, jax.ShapeDtypeStruct((total, width), BF16)],
        compiler_params=params(),
        cost_estimate=cost(10 * total * width * hidden, 6 * local * width * hidden),
        name="backward_experts",
    )(both, both, gate, up, down)


def weight_grads(both, hidden_rows, gate_grad, up_grad, local):
    total, hidden = gate_grad.shape
    width = both.shape[1] // 2
    slots = total // local
    grad_wide = pl.BlockSpec((slots, width), lambda e: (e, 1))
    wide, narrow, column, row = expert_specs(local, slots, width, hidden)
    return pl.pallas_call(
        weights_kernel,
        grid=(local,),
        in_specs=[wide, grad_wide, narrow, narrow, narrow],
        out_specs=[column, column, row],
        out_shape=[
            jax.ShapeDtypeStruct((local, width, hidden), BF16),
            jax.ShapeDtypeStruct((local, width, hidden), BF16),
            jax.ShapeDtypeStruct((local, hidden, width), BF16),
        ],
        compiler_params=params(),
        cost_estimate=cost(6 * total * width * hidden, 6 * local * width * hidden),
        name="weight_grads",
    )(both, both, hidden_rows, gate_grad, up_grad)


def halves(block, dp_index):
    half = block.shape[0] // 2
    mine = lax.dynamic_slice_in_dim(block, dp_index * half, half, 0)
    other = lax.dynamic_slice_in_dim(block, (1 - dp_index) * half, half, 0)
    return mine, other


def spread_near(mine, groups):
    if groups != 4:
        return [lax.all_gather(mine, "expert", tiled=True)]
    return [swap(mine, "expert", 1), swap(mine, "expert", 2)]


def spread_far(near, groups):
    if groups == 4:
        near = near + [swap(near[1], "expert", 1)]
    return near, [swap(piece, "dp", 1) for piece in near]


def pieces(mine, near, other, far, groups):
    if groups != 4:
        return near + far
    return [mine] + near + [other] + far


def spread_meta(meta, dp_index, groups):
    half = meta.shape[0] // 2
    both = jnp.concatenate(halves(meta, dp_index), 0)
    if groups != 4:
        metas = list(lax.all_gather(both, "expert"))
    else:
        metas = [both] + [swap(both, "expert", r) for r in range(1, groups)]
    return jnp.concatenate([m[:half] for m in metas] + [m[half:] for m in metas], 0)


def sums_sent(keep, received, groups):
    pair = (keep.astype(F32) + received.astype(F32)).astype(BF16)
    pair = pair.reshape(groups, keep.shape[0] // groups, -1)
    if groups != 4:
        return [lax.all_to_all(pair, "expert", 0, 0, tiled=True)]
    return [pair[0]] + [swap(pair[r], "expert", r) for r in range(1, groups)]


def sums_home(base, sent):
    total = base.astype(F32)
    for piece in sent:
        piece = piece.astype(F32)
        total = total + (jnp.sum(piece, 0) if piece.ndim == 3 else piece)
    return total.astype(BF16)


def to_section(mine, direction, dp_index):
    n, m = lax.axis_size("section"), lax.axis_size("dp")
    same = rotate(mine, "section", direction)
    route = [
        (s * m + d, ((s + direction) % n) * m + (m - 1 - d)) for s in range(n) for d in range(m)
    ]
    cross = lax.ppermute(mine, ("section", "dp"), route)
    first = jnp.where(dp_index == 0, same, cross)
    second = jnp.where(dp_index == 0, cross, same)
    return jnp.concatenate([first, second], 0)


def slot_tables(meta, choices, base, local):
    tokens = meta.shape[0]
    meta = meta.reshape(tokens, 2, 2, choices)
    routes, counted = meta[:, :, 0], meta[:, :, 1].astype(F32)
    mixing = counted / jnp.sum(counted, -1, keepdims=True)
    hit = (routes[..., None] - base) == jnp.arange(local, dtype=jnp.int32)
    weight = jnp.sum(jnp.where(hit, mixing[..., None], 0.0), 2)
    chosen = jnp.any(hit, 2).astype(jnp.int32)
    rank = jnp.cumsum(chosen, 0) - chosen
    dest = jnp.where(chosen > 0, rank, -1)
    return dest.reshape(tokens, -1), weight.reshape(tokens, -1)


def local(
    fwd_in, fwd_routes, fwd_numer, bwd_saved, bwd_routes, bwd_numer, bwd_grad, w_gate, w_up, w_down
):
    groups = lax.axis_size("expert")
    group, dp_index = lax.axis_index("expert"), lax.axis_index("dp")
    gate, up, down = w_gate[0], w_up[0], w_down[0]
    n_local = gate.shape[0]
    choices = fwd_routes.shape[-1]
    slots = -(-groups * MOST // 16) * 16

    meta = jnp.concatenate([fwd_routes[0], fwd_numer[0], bwd_routes[0], bwd_numer[0]], -1)
    meta_all = spread_meta(meta, dp_index, groups)
    dest, weight = slot_tables(meta_all, choices, group * n_local, n_local)

    in_mine, in_other = halves(fwd_in[0], dp_index)
    grad_mine, _ = halves(bwd_grad[0], dp_index)
    back_mine, back_other = halves(jnp.concatenate([bwd_saved[0], bwd_grad[0]], 1), dp_index)

    near = spread_near(in_mine, groups)
    back_near = spread_near(after(back_mine, *near), groups)
    near, far = spread_far(near, groups)

    ordered, back_ordered, mix, back_mix, slot_weight = routing_matrices(dest, weight, slots)
    in_rows = in_expert_order(ordered, pieces(in_mine, near, in_other, far, groups))
    in_rows, *back_near = lax.optimization_barrier((in_rows, *back_near))
    back_near, back_far = spread_far(back_near, groups)
    out_rows = forward_experts(in_rows, gate, up, down)
    out_keep, out_send = token_sums(mix, out_rows, 0, 1)
    out_received = swap(after(out_send, back_far[-1]), "dp", 1)

    back_rows = in_expert_order(
        back_ordered, pieces(back_mine, back_near, back_other, back_far, groups), slot_weight
    )
    hidden, gate_grad, up_grad, row_grad = backward_experts(back_rows, gate, up, down)
    row_grad, out_received = lax.optimization_barrier((row_grad, out_received))
    out_sent = sums_sent(out_keep, out_received, groups)
    keep, send = token_sums(back_mix, row_grad, 0, 1)
    received = swap(send, "dp", 1)
    gate_grad = after(gate_grad, keep)
    gate_sum, up_sum, down_sum = weight_grads(back_rows, hidden, gate_grad, up_grad, n_local)
    gate_sum, received, *out_sent = lax.optimization_barrier((gate_sum, received, *out_sent))
    sent = sums_sent(keep, received, groups)
    next_fwd = to_section(sums_home(in_mine, out_sent), 1, dp_index)
    next_bwd = to_section(sums_home(grad_mine, sent), -1, dp_index)
    return (next_fwd[None], next_bwd[None], gate_sum[None], up_sum[None], down_sum[None])


def solution(mesh):
    in_specs = (
        P("section", "expert", None),
        P("section", "expert", None),
        P("section", "expert", None),
        P("section", "expert", None),
        P("section", "expert", None),
        P("section", "expert", None),
        P("section", "expert", None),
        P("section", "expert", None, "dp"),
        P("section", "expert", None, "dp"),
        P("section", "expert", "dp", None),
    )
    out_specs = (
        P("section", "expert", None),
        P("section", "expert", None),
        P("section", "expert", None, "dp"),
        P("section", "expert", None, "dp"),
        P("section", "expert", "dp", None),
    )
    return jax.shard_map(local, mesh=mesh, in_specs=in_specs, out_specs=out_specs, check_vma=False)
```

```python
import functools

import jax
import jax.numpy as jnp
from jax import lax
from jax.experimental import pallas as pl
from jax.experimental.pallas import tpu as pltpu
from jax.sharding import PartitionSpec as P

EXPERTS = 32
MOST = 26
BF16 = jnp.bfloat16
F32 = jnp.float32
MIB = 1 << 20

NN = (((1,), (0,)), ((), ()))
NT = (((1,), (1,)), ((), ()))
TN = (((0,), (0,)), ((), ()))


def dot(a, b, dims=NN):
    return lax.dot_general(a, b, dims, preferred_element_type=F32)


def rotate(block, axis, distance):
    n = lax.axis_size(axis)
    return lax.ppermute(block, axis, [(i, (i + distance) % n) for i in range(n)])


def swap(block, axis, mask):
    n = lax.axis_size(axis)
    return lax.ppermute(block, axis, [(i, i ^ mask) for i in range(n)])


def after(value, *others):
    return lax.optimization_barrier((value, *others))[0]


def params(slots):
    return pltpu.CompilerParams(vmem_limit_bytes=(40 if slots <= 128 else 48) * MIB)


def cost(flops, nbytes):
    return pl.CostEstimate(flops=int(flops), bytes_accessed=int(nbytes), transcendentals=0)


def routing_kernel(slots, dest_ref, weight_ref, dest_col_ref, weight_col_ref, *refs):
    ordered_refs, mix_refs, slot_weight_ref = refs[:2], refs[2:4], refs[4]
    total, tokens = ordered_refs[0].shape
    local = total // slots
    place = lax.broadcasted_iota(jnp.int32, (slots, tokens), 0)
    slot = lax.broadcasted_iota(jnp.int32, (tokens, total), 1)
    for way in range(2):
        mix = jnp.zeros((tokens, total), F32)
        for l in range(local):
            at = way * local + l
            part = slice(l * slots, (l + 1) * slots)
            hit = place == dest_ref[at : at + 1, :]
            ordered_refs[way][part, :] = jnp.where(hit, 1.0, 0.0).astype(BF16)
            if way == 1:
                slot_weight_ref[part, :] = jnp.sum(
                    jnp.where(hit, weight_ref[at : at + 1, :], 0.0), 1, keepdims=True
                )
            here = dest_col_ref[:, at : at + 1]
            here = jnp.where(here >= 0, here + l * slots, -1)
            value = weight_col_ref[:, at : at + 1] if way == 0 else 1.0
            mix = jnp.where(slot == here, value, mix)
        mix_refs[way][...] = mix.astype(BF16)


def routing_matrices(dest, weight, slots):
    tokens, both = dest.shape
    total = both // 2 * slots
    return pl.pallas_call(
        functools.partial(routing_kernel, slots),
        out_shape=[jax.ShapeDtypeStruct((total, tokens), BF16)] * 2
        + [jax.ShapeDtypeStruct((tokens, total), BF16)] * 2
        + [jax.ShapeDtypeStruct((total, 1), F32)],
        compiler_params=params(slots),
        cost_estimate=cost(0, 8 * total * tokens),
        name="routing",
    )(dest.T, weight.T, dest, weight)


def order_kernel(n_pieces, onehot_ref, *refs):
    *pieces, out_ref, rows_ref = refs
    at = 0
    for piece in pieces:
        rows_ref[at : at + piece.shape[0], :] = piece[...]
        at += piece.shape[0]
    out_ref[...] = dot(onehot_ref[...], rows_ref[...]).astype(BF16)


def weighted_order_kernel(n_pieces, plain, onehot_ref, slot_weight_ref, *refs):
    *pieces, out_ref, rows_ref = refs
    at = 0
    for piece in pieces:
        rows_ref[at : at + piece.shape[0], :] = piece[...]
        at += piece.shape[0]
    ordered = dot(onehot_ref[...], rows_ref[...])
    scale = jnp.where(pl.program_id(0) < plain, 1.0, slot_weight_ref[...])
    out_ref[...] = (ordered * scale).astype(BF16)


def in_expert_order(onehot, pieces, slot_weight=None):
    total, tokens = onehot.shape
    width = pieces[0].shape[1]
    chunk = min(512, width)
    steps = width // chunk
    in_specs = [pl.BlockSpec((total, tokens), lambda c: (0, 0))]
    operands = [onehot]
    if slot_weight is None:
        kernel = functools.partial(order_kernel, len(pieces))
    else:
        kernel = functools.partial(weighted_order_kernel, len(pieces), steps // 2)
        in_specs.append(pl.BlockSpec((total, 1), lambda c: (0, 0)))
        operands.append(slot_weight)
    in_specs += [pl.BlockSpec((piece.shape[0], chunk), lambda c: (0, c)) for piece in pieces]
    return pl.pallas_call(
        kernel,
        grid=(steps,),
        in_specs=in_specs,
        out_specs=pl.BlockSpec((total, chunk), lambda c: (0, c)),
        out_shape=jax.ShapeDtypeStruct((total, width), BF16),
        scratch_shapes=[pltpu.VMEM((tokens, chunk), BF16)],
        compiler_params=params(total // 8),
        cost_estimate=cost(2 * total * tokens * width, 2 * (total + tokens) * width),
        name="order_rows",
    )(*operands, *pieces)


def combine_kernel(mix_ref, rows_ref, keep_ref, send_ref):
    half = mix_ref.shape[0] // 2
    summed = dot(mix_ref[...], rows_ref[...]).astype(BF16)
    keep_ref[...] = summed[:half]
    send_ref[...] = summed[half:]


def token_sums(mix, rows, part, parts):
    tokens, total = mix.shape
    width = rows.shape[1] // parts
    chunk = min(512, width)
    steps = width // chunk
    return pl.pallas_call(
        combine_kernel,
        grid=(steps,),
        in_specs=[
            pl.BlockSpec((tokens, total), lambda c: (0, 0)),
            pl.BlockSpec((total, chunk), lambda c: (0, c + part * steps)),
        ],
        out_specs=[pl.BlockSpec((tokens // 2, chunk), lambda c: (0, c))] * 2,
        out_shape=[jax.ShapeDtypeStruct((tokens // 2, width), BF16)] * 2,
        compiler_params=params(total // 8),
        cost_estimate=cost(2 * total * tokens * width, 2 * (total + tokens) * width),
        name="token_sums",
    )(mix, rows)


def forward_kernel(rows_ref, gate_ref, up_ref, down_ref, out_ref):
    rows = rows_ref[...]
    gate_value = dot(rows, gate_ref[0])
    up_value = dot(rows, up_ref[0])
    hidden = (gate_value / (1.0 + jnp.exp(-gate_value)) * up_value).astype(BF16)
    out_ref[...] = dot(hidden, down_ref[0]).astype(BF16)


def backward_kernel(
    rows_ref, grad_ref, gate_ref, up_ref, down_ref, hidden_ref, gate_grad_ref, up_grad_ref, out_ref
):
    rows = rows_ref[...]
    gate_value = dot(rows, gate_ref[0])
    up_value = dot(rows, up_ref[0])
    hidden_grad = dot(grad_ref[...], down_ref[0], NT)
    sig = 1.0 / (1.0 + jnp.exp(-gate_value))
    silu = gate_value * sig
    hidden_ref[...] = (silu * up_value).astype(BF16)
    up_grad = (hidden_grad * silu).astype(BF16)
    gate_grad = (hidden_grad * up_value * sig * (1.0 + gate_value * (1.0 - sig))).astype(BF16)
    up_grad_ref[...] = up_grad
    gate_grad_ref[...] = gate_grad
    out_ref[...] = (dot(gate_grad, gate_ref[0], NT) + dot(up_grad, up_ref[0], NT)).astype(BF16)


def weights_kernel(
    rows_ref, grad_ref, hidden_ref, gate_grad_ref, up_grad_ref, gate_ref, up_ref, down_ref
):
    rows = rows_ref[...]
    gate_ref[0] = dot(rows, gate_grad_ref[...], TN).astype(BF16)
    up_ref[0] = dot(rows, up_grad_ref[...], TN).astype(BF16)
    down_ref[0] = dot(hidden_ref[...], grad_ref[...], TN).astype(BF16)


def expert_specs(local, slots, width, hidden):
    wide = pl.BlockSpec((slots, width), lambda e: (e, 0))
    narrow = pl.BlockSpec((slots, hidden), lambda e: (e, 0))
    column = pl.BlockSpec((1, width, hidden), lambda e: (e, 0, 0))
    row = pl.BlockSpec((1, hidden, width), lambda e: (e, 0, 0))
    return wide, narrow, column, row


def forward_experts(rows, gate, up, down):
    local, width, hidden = gate.shape
    slots = rows.shape[0] // local
    wide, narrow, column, row = expert_specs(local, slots, width, hidden)
    return pl.pallas_call(
        forward_kernel,
        grid=(local,),
        in_specs=[wide, column, column, row],
        out_specs=wide,
        out_shape=jax.ShapeDtypeStruct(rows.shape, BF16),
        compiler_params=params(slots),
        cost_estimate=cost(6 * rows.shape[0] * width * hidden, 6 * local * width * hidden),
        name="forward_experts",
    )(rows, gate, up, down)


def backward_experts(both, gate, up, down):
    local, width, hidden = gate.shape
    total = both.shape[0]
    slots = total // local
    wide, narrow, column, row = expert_specs(local, slots, width, hidden)
    grad_wide = pl.BlockSpec((slots, width), lambda e: (e, 1))
    small = jax.ShapeDtypeStruct((total, hidden), BF16)
    return pl.pallas_call(
        backward_kernel,
        grid=(local,),
        in_specs=[wide, grad_wide, column, column, row],
        out_specs=[narrow, narrow, narrow, wide],
        out_shape=[small, small, small, jax.ShapeDtypeStruct((total, width), BF16)],
        compiler_params=params(slots),
        cost_estimate=cost(10 * total * width * hidden, 6 * local * width * hidden),
        name="backward_experts",
    )(both, both, gate, up, down)


def weight_grads(both, hidden_rows, gate_grad, up_grad, local):
    total, hidden = gate_grad.shape
    width = both.shape[1] // 2
    slots = total // local
    grad_wide = pl.BlockSpec((slots, width), lambda e: (e, 1))
    wide, narrow, column, row = expert_specs(local, slots, width, hidden)
    return pl.pallas_call(
        weights_kernel,
        grid=(local,),
        in_specs=[wide, grad_wide, narrow, narrow, narrow],
        out_specs=[column, column, row],
        out_shape=[
            jax.ShapeDtypeStruct((local, width, hidden), BF16),
            jax.ShapeDtypeStruct((local, width, hidden), BF16),
            jax.ShapeDtypeStruct((local, hidden, width), BF16),
        ],
        compiler_params=params(slots),
        cost_estimate=cost(6 * total * width * hidden, 6 * local * width * hidden),
        name="weight_grads",
    )(both, both, hidden_rows, gate_grad, up_grad)


def halves(block, dp_index):
    half = block.shape[0] // 2
    mine = lax.dynamic_slice_in_dim(block, dp_index * half, half, 0)
    other = lax.dynamic_slice_in_dim(block, (1 - dp_index) * half, half, 0)
    return mine, other


def cross(block, axis, mask):
    n, m = lax.axis_size(axis), lax.axis_size("dp")
    route = [(i * m + d, (i ^ mask) * m + (m - 1 - d)) for i in range(n) for d in range(m)]
    return lax.ppermute(block, (axis, "dp"), route)


def spread_meta(meta, dp_index, groups):
    half = meta.shape[0] // 2
    both = jnp.concatenate(halves(meta, dp_index), 0)
    if groups != 4:
        metas = list(lax.all_gather(both, "expert"))
    else:
        metas = [both] + [swap(both, "expert", r) for r in range(1, groups)]
    return jnp.concatenate([m[:half] for m in metas] + [m[half:] for m in metas], 0)


def sums_sent(keep, received, groups):
    pair = (keep.astype(F32) + received.astype(F32)).astype(BF16)
    pair = pair.reshape(groups, keep.shape[0] // groups, -1)
    if groups != 4:
        return [lax.all_to_all(pair, "expert", 0, 0, tiled=True)]
    return [pair[0]] + [swap(pair[r], "expert", r) for r in range(1, groups)]


def sums_home(base, sent):
    total = base.astype(F32)
    for piece in sent:
        piece = piece.astype(F32)
        total = total + (jnp.sum(piece, 0) if piece.ndim == 3 else piece)
    return total.astype(BF16)


def to_section(mine, direction, dp_index):
    n, m = lax.axis_size("section"), lax.axis_size("dp")
    same = rotate(mine, "section", direction)
    route = [
        (s * m + d, ((s + direction) % n) * m + (m - 1 - d)) for s in range(n) for d in range(m)
    ]
    other = lax.ppermute(mine, ("section", "dp"), route)
    first = jnp.where(dp_index == 0, same, other)
    second = jnp.where(dp_index == 0, other, same)
    return jnp.concatenate([first, second], 0)


def slot_tables(meta, choices, base, local):
    tokens = meta.shape[0]
    meta = meta.reshape(tokens, 2, 2, choices)
    routes, counted = meta[:, :, 0], meta[:, :, 1].astype(F32)
    mixing = counted / jnp.sum(counted, -1, keepdims=True)
    hit = (routes[..., None] - base) == jnp.arange(local, dtype=jnp.int32)
    weight = jnp.sum(jnp.where(hit, mixing[..., None], 0.0), 2)
    chosen = jnp.any(hit, 2).astype(jnp.int32)
    rank = jnp.cumsum(chosen, 0) - chosen
    dest = jnp.where(chosen > 0, rank, -1)
    return dest.reshape(tokens, -1), weight.reshape(tokens, -1)


def local(
    fwd_in, fwd_routes, fwd_numer, bwd_saved, bwd_routes, bwd_numer, bwd_grad, w_gate, w_up, w_down
):
    groups = lax.axis_size("expert")
    group, dp_index = lax.axis_index("expert"), lax.axis_index("dp")
    gate, up, down = w_gate[0], w_up[0], w_down[0]
    n_local = gate.shape[0]
    choices = fwd_routes.shape[-1]
    slots = -(-groups * MOST // 16) * 16

    meta = jnp.concatenate([fwd_routes[0], fwd_numer[0], bwd_routes[0], bwd_numer[0]], -1)
    in_mine, in_other = halves(fwd_in[0], dp_index)
    meta_all = spread_meta(after(meta, in_mine), dp_index, groups)
    dest, weight = slot_tables(meta_all, choices, group * n_local, n_local)
    grad_mine, _ = halves(bwd_grad[0], dp_index)
    back_mine, back_other = halves(jnp.concatenate([bwd_saved[0], bwd_grad[0]], 1), dp_index)

    if groups == 4:
        near, past = swap(in_mine, "expert", 1), swap(in_mine, "expert", 2)
        back_near = swap(after(back_mine, near, past), "expert", 1)
        last = swap(past, "expert", 1)
        far = [swap(near, "dp", 1), swap(past, "dp", 1), swap(last, "dp", 1)]
        back_past = swap(after(back_mine, last), "expert", 2)
        in_pieces = [in_mine, near, past, last, in_other, *far]
    else:
        near = lax.all_gather(in_mine, "expert", tiled=True)
        back_near = lax.all_gather(back_mine, "expert", tiled=True)
        back_past = ()
        in_pieces = [near, swap(near, "dp", 1)]

    ordered, back_ordered, mix, back_mix, slot_weight = routing_matrices(dest, weight, slots)
    ordered, back_near = lax.optimization_barrier((ordered, back_near))
    back_far = swap(back_near, "dp", 1)
    in_rows = in_expert_order(ordered, in_pieces)
    in_rows, back_past = lax.optimization_barrier((in_rows, back_past))
    if groups == 4:
        back_last = swap(back_past, "expert", 1)
        back_far = [back_far, swap(back_past, "dp", 1), cross(back_past, "expert", 1)]
        back_pieces = [back_mine, back_near, back_past, back_last, back_other, *back_far]
    else:
        back_pieces = [back_near, back_far]
    out_rows = forward_experts(in_rows, gate, up, down)
    out_keep, out_send = token_sums(mix, out_rows, 0, 1)
    out_received = swap(after(out_send, back_pieces[-1]), "dp", 1)

    back_rows = in_expert_order(back_ordered, back_pieces, slot_weight)
    hidden, gate_grad, up_grad, row_grad = backward_experts(back_rows, gate, up, down)
    row_grad, out_received = lax.optimization_barrier((row_grad, out_received))
    out_sent = sums_sent(out_keep, out_received, groups)
    keep, send = token_sums(back_mix, row_grad, 0, 1)
    received = swap(send, "dp", 1)
    gate_grad = after(gate_grad, keep)
    gate_sum, up_sum, down_sum = weight_grads(back_rows, hidden, gate_grad, up_grad, n_local)
    gate_sum, received, *out_sent = lax.optimization_barrier((gate_sum, received, *out_sent))
    sent = sums_sent(keep, received, groups)
    next_fwd = to_section(sums_home(in_mine, out_sent), 1, dp_index)
    next_bwd = to_section(sums_home(grad_mine, sent), -1, dp_index)
    return (next_fwd[None], next_bwd[None], gate_sum[None], up_sum[None], down_sum[None])


def solution(mesh):
    in_specs = (
        P("section", "expert", None),
        P("section", "expert", None),
        P("section", "expert", None),
        P("section", "expert", None),
        P("section", "expert", None),
        P("section", "expert", None),
        P("section", "expert", None),
        P("section", "expert", None, "dp"),
        P("section", "expert", None, "dp"),
        P("section", "expert", "dp", None),
    )
    out_specs = (
        P("section", "expert", None),
        P("section", "expert", None),
        P("section", "expert", None, "dp"),
        P("section", "expert", None, "dp"),
        P("section", "expert", "dp", None),
    )
    return jax.shard_map(local, mesh=mesh, in_specs=in_specs, out_specs=out_specs, check_vma=False)
```

```python
import functools

import jax
import jax.numpy as jnp
from jax import lax
from jax.experimental import pallas as pl
from jax.experimental.pallas import tpu as pltpu
from jax.sharding import PartitionSpec as P

EXPERTS = 32
MOST = 26
BF16 = jnp.bfloat16
F32 = jnp.float32
MIB = 1 << 20

NN = (((1,), (0,)), ((), ()))
NT = (((1,), (1,)), ((), ()))
TN = (((0,), (0,)), ((), ()))


def dot(a, b, dims=NN):
    return lax.dot_general(a, b, dims, preferred_element_type=F32)


def rotate(block, axis, distance):
    n = lax.axis_size(axis)
    return lax.ppermute(block, axis, [(i, (i + distance) % n) for i in range(n)])


def swap(block, axis, mask):
    n = lax.axis_size(axis)
    return lax.ppermute(block, axis, [(i, i ^ mask) for i in range(n)])


def after(value, *others):
    return lax.optimization_barrier((value, *others))[0]


def params(slots):
    return pltpu.CompilerParams(vmem_limit_bytes=(40 if slots <= 128 else 48) * MIB)


def cost(flops, nbytes):
    return pl.CostEstimate(flops=int(flops), bytes_accessed=int(nbytes), transcendentals=0)


def routing_kernel(slots, dest_ref, weight_ref, dest_col_ref, weight_col_ref, *refs):
    ordered_refs, mix_refs, slot_weight_ref = refs[:2], refs[2:4], refs[4]
    total, tokens = ordered_refs[0].shape
    local = total // slots
    place = lax.broadcasted_iota(jnp.int32, (slots, tokens), 0)
    slot = lax.broadcasted_iota(jnp.int32, (tokens, total), 1)
    for way in range(2):
        mix = jnp.zeros((tokens, total), F32)
        for l in range(local):
            at = way * local + l
            part = slice(l * slots, (l + 1) * slots)
            hit = place == dest_ref[at : at + 1, :]
            ordered_refs[way][part, :] = jnp.where(hit, 1.0, 0.0).astype(BF16)
            if way == 1:
                slot_weight_ref[part, :] = jnp.sum(
                    jnp.where(hit, weight_ref[at : at + 1, :], 0.0), 1, keepdims=True
                )
            here = dest_col_ref[:, at : at + 1]
            here = jnp.where(here >= 0, here + l * slots, -1)
            value = weight_col_ref[:, at : at + 1] if way == 0 else 1.0
            mix = jnp.where(slot == here, value, mix)
        mix_refs[way][...] = mix.astype(BF16)


def routing_matrices(dest, weight, slots):
    tokens, both = dest.shape
    total = both // 2 * slots
    return pl.pallas_call(
        functools.partial(routing_kernel, slots),
        out_shape=[jax.ShapeDtypeStruct((total, tokens), BF16)] * 2
        + [jax.ShapeDtypeStruct((tokens, total), BF16)] * 2
        + [jax.ShapeDtypeStruct((total, 1), F32)],
        compiler_params=params(slots),
        cost_estimate=cost(0, 8 * total * tokens),
        name="routing",
    )(dest.T, weight.T, dest, weight)


def order_kernel(n_pieces, onehot_ref, *refs):
    *pieces, out_ref, rows_ref = refs
    at = 0
    for piece in pieces:
        rows_ref[at : at + piece.shape[0], :] = piece[...]
        at += piece.shape[0]
    out_ref[...] = dot(onehot_ref[...], rows_ref[...]).astype(BF16)


def weighted_order_kernel(n_pieces, plain, onehot_ref, slot_weight_ref, *refs):
    *pieces, out_ref, rows_ref = refs
    at = 0
    for piece in pieces:
        rows_ref[at : at + piece.shape[0], :] = piece[...]
        at += piece.shape[0]
    ordered = dot(onehot_ref[...], rows_ref[...])
    scale = jnp.where(pl.program_id(0) < plain, 1.0, slot_weight_ref[...])
    out_ref[...] = (ordered * scale).astype(BF16)


def in_expert_order(onehot, pieces, slot_weight=None):
    total, tokens = onehot.shape
    width = pieces[0].shape[1]
    chunk = min(2048 if tokens <= 512 else 512, width)
    steps = width // chunk
    in_specs = [pl.BlockSpec((total, tokens), lambda c: (0, 0))]
    operands = [onehot]
    if slot_weight is None:
        kernel = functools.partial(order_kernel, len(pieces))
    else:
        kernel = functools.partial(weighted_order_kernel, len(pieces), steps // 2)
        in_specs.append(pl.BlockSpec((total, 1), lambda c: (0, 0)))
        operands.append(slot_weight)
    in_specs += [pl.BlockSpec((piece.shape[0], chunk), lambda c: (0, c)) for piece in pieces]
    return pl.pallas_call(
        kernel,
        grid=(steps,),
        in_specs=in_specs,
        out_specs=pl.BlockSpec((total, chunk), lambda c: (0, c)),
        out_shape=jax.ShapeDtypeStruct((total, width), BF16),
        scratch_shapes=[pltpu.VMEM((tokens, chunk), BF16)],
        compiler_params=params(total // 8),
        cost_estimate=cost(2 * total * tokens * width, 2 * (total + tokens) * width),
        name="order_rows",
    )(*operands, *pieces)


def combine_kernel(mix_ref, rows_ref, keep_ref, send_ref):
    half = mix_ref.shape[0] // 2
    summed = dot(mix_ref[...], rows_ref[...]).astype(BF16)
    keep_ref[...] = summed[:half]
    send_ref[...] = summed[half:]


def token_sums(mix, rows, part, parts):
    tokens, total = mix.shape
    width = rows.shape[1] // parts
    chunk = min(2048 if tokens <= 512 else 512, width)
    steps = width // chunk
    return pl.pallas_call(
        combine_kernel,
        grid=(steps,),
        in_specs=[
            pl.BlockSpec((tokens, total), lambda c: (0, 0)),
            pl.BlockSpec((total, chunk), lambda c: (0, c + part * steps)),
        ],
        out_specs=[pl.BlockSpec((tokens // 2, chunk), lambda c: (0, c))] * 2,
        out_shape=[jax.ShapeDtypeStruct((tokens // 2, width), BF16)] * 2,
        compiler_params=params(total // 8),
        cost_estimate=cost(2 * total * tokens * width, 2 * (total + tokens) * width),
        name="token_sums",
    )(mix, rows)


def forward_kernel(rows_ref, gate_ref, up_ref, down_ref, out_ref):
    rows = rows_ref[...]
    gate_value = dot(rows, gate_ref[0])
    up_value = dot(rows, up_ref[0])
    hidden = (gate_value / (1.0 + jnp.exp(-gate_value)) * up_value).astype(BF16)
    out_ref[...] = dot(hidden, down_ref[0]).astype(BF16)


def backward_kernel(
    rows_ref, grad_ref, gate_ref, up_ref, down_ref, hidden_ref, gate_grad_ref, up_grad_ref, out_ref
):
    rows = rows_ref[...]
    gate_value = dot(rows, gate_ref[0])
    up_value = dot(rows, up_ref[0])
    hidden_grad = dot(grad_ref[...], down_ref[0], NT)
    sig = 1.0 / (1.0 + jnp.exp(-gate_value))
    silu = gate_value * sig
    hidden_ref[...] = (silu * up_value).astype(BF16)
    up_grad = (hidden_grad * silu).astype(BF16)
    gate_grad = (hidden_grad * up_value * sig * (1.0 + gate_value * (1.0 - sig))).astype(BF16)
    up_grad_ref[...] = up_grad
    gate_grad_ref[...] = gate_grad
    width = out_ref.shape[1]
    for at in range(0, width, 512):
        part = slice(at, min(at + 512, width))
        row_grad = dot(gate_grad, gate_ref[0, part], NT) + dot(up_grad, up_ref[0, part], NT)
        out_ref[:, part] = row_grad.astype(BF16)


def weights_kernel(
    rows_ref, grad_ref, hidden_ref, gate_grad_ref, up_grad_ref, gate_ref, up_ref, down_ref
):
    rows = rows_ref[...]
    gate_ref[0] = dot(rows, gate_grad_ref[...], TN).astype(BF16)
    up_ref[0] = dot(rows, up_grad_ref[...], TN).astype(BF16)
    down_ref[0] = dot(hidden_ref[...], grad_ref[...], TN).astype(BF16)


def expert_specs(local, slots, width, hidden):
    wide = pl.BlockSpec((slots, width), lambda e: (e, 0))
    narrow = pl.BlockSpec((slots, hidden), lambda e: (e, 0))
    column = pl.BlockSpec((1, width, hidden), lambda e: (e, 0, 0))
    row = pl.BlockSpec((1, hidden, width), lambda e: (e, 0, 0))
    return wide, narrow, column, row


def forward_experts(rows, gate, up, down):
    local, width, hidden = gate.shape
    slots = rows.shape[0] // local
    wide, narrow, column, row = expert_specs(local, slots, width, hidden)
    return pl.pallas_call(
        forward_kernel,
        grid=(local,),
        in_specs=[wide, column, column, row],
        out_specs=wide,
        out_shape=jax.ShapeDtypeStruct(rows.shape, BF16),
        compiler_params=params(slots),
        cost_estimate=cost(6 * rows.shape[0] * width * hidden, 6 * local * width * hidden),
        name="forward_experts",
    )(rows, gate, up, down)


def backward_experts(both, gate, up, down):
    local, width, hidden = gate.shape
    total = both.shape[0]
    slots = total // local
    wide, narrow, column, row = expert_specs(local, slots, width, hidden)
    grad_wide = pl.BlockSpec((slots, width), lambda e: (e, 1))
    small = jax.ShapeDtypeStruct((total, hidden), BF16)
    return pl.pallas_call(
        backward_kernel,
        grid=(local,),
        in_specs=[wide, grad_wide, column, column, row],
        out_specs=[narrow, narrow, narrow, wide],
        out_shape=[small, small, small, jax.ShapeDtypeStruct((total, width), BF16)],
        compiler_params=params(slots),
        cost_estimate=cost(10 * total * width * hidden, 6 * local * width * hidden),
        name="backward_experts",
    )(both, both, gate, up, down)


def weight_grads(both, hidden_rows, gate_grad, up_grad, local):
    total, hidden = gate_grad.shape
    width = both.shape[1] // 2
    slots = total // local
    grad_wide = pl.BlockSpec((slots, width), lambda e: (e, 1))
    wide, narrow, column, row = expert_specs(local, slots, width, hidden)
    return pl.pallas_call(
        weights_kernel,
        grid=(local,),
        in_specs=[wide, grad_wide, narrow, narrow, narrow],
        out_specs=[column, column, row],
        out_shape=[
            jax.ShapeDtypeStruct((local, width, hidden), BF16),
            jax.ShapeDtypeStruct((local, width, hidden), BF16),
            jax.ShapeDtypeStruct((local, hidden, width), BF16),
        ],
        compiler_params=params(slots),
        cost_estimate=cost(6 * total * width * hidden, 6 * local * width * hidden),
        name="weight_grads",
    )(both, both, hidden_rows, gate_grad, up_grad)


def halves(block, dp_index):
    half = block.shape[0] // 2
    mine = lax.dynamic_slice_in_dim(block, dp_index * half, half, 0)
    other = lax.dynamic_slice_in_dim(block, (1 - dp_index) * half, half, 0)
    return mine, other


def cross(block, axis, mask):
    n, m = lax.axis_size(axis), lax.axis_size("dp")
    route = [(i * m + d, (i ^ mask) * m + (m - 1 - d)) for i in range(n) for d in range(m)]
    return lax.ppermute(block, (axis, "dp"), route)


def spread_meta(meta, dp_index, groups):
    half = meta.shape[0] // 2
    both = jnp.concatenate(halves(meta, dp_index), 0)
    if groups != 4:
        metas = list(lax.all_gather(both, "expert"))
    else:
        metas = [both] + [swap(both, "expert", r) for r in range(1, groups)]
    return jnp.concatenate([m[:half] for m in metas] + [m[half:] for m in metas], 0)


def sums_sent(keep, received, groups):
    pair = (keep.astype(F32) + received.astype(F32)).astype(BF16)
    pair = pair.reshape(groups, keep.shape[0] // groups, -1)
    if groups != 4:
        return [lax.all_to_all(pair, "expert", 0, 0, tiled=True)]
    return [pair[0]] + [swap(pair[r], "expert", r) for r in range(1, groups)]


def sums_home(base, sent):
    total = base.astype(F32)
    for piece in sent:
        piece = piece.astype(F32)
        total = total + (jnp.sum(piece, 0) if piece.ndim == 3 else piece)
    return total.astype(BF16)


def to_section(mine, direction, dp_index):
    n, m = lax.axis_size("section"), lax.axis_size("dp")
    same = rotate(mine, "section", direction)
    route = [
        (s * m + d, ((s + direction) % n) * m + (m - 1 - d)) for s in range(n) for d in range(m)
    ]
    other = lax.ppermute(mine, ("section", "dp"), route)
    first = jnp.where(dp_index == 0, same, other)
    second = jnp.where(dp_index == 0, other, same)
    return jnp.concatenate([first, second], 0)


def slot_tables(meta, choices, base, local):
    tokens = meta.shape[0]
    meta = meta.reshape(tokens, 2, 2, choices)
    routes, counted = meta[:, :, 0], meta[:, :, 1].astype(F32)
    mixing = counted / jnp.sum(counted, -1, keepdims=True)
    hit = (routes[..., None] - base) == jnp.arange(local, dtype=jnp.int32)
    weight = jnp.sum(jnp.where(hit, mixing[..., None], 0.0), 2)
    chosen = jnp.any(hit, 2).astype(jnp.int32)
    rank = jnp.cumsum(chosen, 0) - chosen
    dest = jnp.where(chosen > 0, rank, -1)
    return dest.reshape(tokens, -1), weight.reshape(tokens, -1)


def local(
    fwd_in, fwd_routes, fwd_numer, bwd_saved, bwd_routes, bwd_numer, bwd_grad, w_gate, w_up, w_down
):
    groups = lax.axis_size("expert")
    group, dp_index = lax.axis_index("expert"), lax.axis_index("dp")
    gate, up, down = w_gate[0], w_up[0], w_down[0]
    n_local = gate.shape[0]
    choices = fwd_routes.shape[-1]
    slots = -(-groups * MOST // 16) * 16

    meta = jnp.concatenate([fwd_routes[0], fwd_numer[0], bwd_routes[0], bwd_numer[0]], -1)
    in_mine, in_other = halves(fwd_in[0], dp_index)
    back_mine, back_other = halves(jnp.concatenate([bwd_saved[0], bwd_grad[0]], 1), dp_index)
    meta_all = spread_meta(after(meta, back_mine), dp_index, groups)
    dest, weight = slot_tables(meta_all, choices, group * n_local, n_local)
    grad_mine, _ = halves(bwd_grad[0], dp_index)

    if groups == 4:
        near, past = swap(in_mine, "expert", 1), swap(after(in_mine, back_mine), "expert", 2)
        back_near = swap(after(back_mine, near, past), "expert", 1)
        last = swap(past, "expert", 1)
        far = [swap(near, "dp", 1), swap(past, "dp", 1), swap(last, "dp", 1)]
        back_past = swap(after(back_mine, last), "expert", 2)
        in_pieces = [in_mine, near, past, last, in_other, *far]
    else:
        near = lax.all_gather(in_mine, "expert", tiled=True)
        back_near = lax.all_gather(back_mine, "expert", tiled=True)
        back_past = ()
        in_pieces = [near, swap(near, "dp", 1)]

    ordered, back_ordered, mix, back_mix, slot_weight = routing_matrices(dest, weight, slots)
    ordered, back_near = lax.optimization_barrier((ordered, back_near))
    back_far = swap(back_near, "dp", 1)
    in_rows = in_expert_order(ordered, in_pieces)
    in_rows, back_past = lax.optimization_barrier((in_rows, back_past))
    if groups == 4:
        back_last = swap(back_past, "expert", 1)
        back_far = [back_far, swap(back_past, "dp", 1), cross(back_past, "expert", 1)]
        back_pieces = [back_mine, back_near, back_past, back_last, back_other, *back_far]
    else:
        back_pieces = [back_near, back_far]
    out_rows = forward_experts(in_rows, gate, up, down)
    out_keep, out_send = token_sums(mix, out_rows, 0, 1)
    out_received = swap(after(out_send, back_pieces[-1]), "dp", 1)

    back_rows = in_expert_order(back_ordered, back_pieces, slot_weight)
    hidden, gate_grad, up_grad, row_grad = backward_experts(back_rows, gate, up, down)
    row_grad, out_received = lax.optimization_barrier((row_grad, out_received))
    out_sent = sums_sent(out_keep, out_received, groups)
    keep, send = token_sums(back_mix, row_grad, 0, 1)
    received = swap(send, "dp", 1)
    gate_grad = after(gate_grad, keep)
    gate_sum, up_sum, down_sum = weight_grads(back_rows, hidden, gate_grad, up_grad, n_local)
    gate_sum, received, *out_sent = lax.optimization_barrier((gate_sum, received, *out_sent))
    sent = sums_sent(keep, received, groups)
    next_fwd = to_section(sums_home(in_mine, out_sent), 1, dp_index)
    next_bwd = to_section(sums_home(grad_mine, sent), -1, dp_index)
    return (next_fwd[None], next_bwd[None], gate_sum[None], up_sum[None], down_sum[None])


def solution(mesh):
    in_specs = (
        P("section", "expert", None),
        P("section", "expert", None),
        P("section", "expert", None),
        P("section", "expert", None),
        P("section", "expert", None),
        P("section", "expert", None),
        P("section", "expert", None),
        P("section", "expert", None, "dp"),
        P("section", "expert", None, "dp"),
        P("section", "expert", "dp", None),
    )
    out_specs = (
        P("section", "expert", None),
        P("section", "expert", None),
        P("section", "expert", None, "dp"),
        P("section", "expert", None, "dp"),
        P("section", "expert", "dp", None),
    )
    return jax.shard_map(local, mesh=mesh, in_specs=in_specs, out_specs=out_specs, check_vma=False)
```

```python
import functools

import jax
import jax.numpy as jnp
from jax import lax
from jax.experimental import pallas as pl
from jax.experimental.pallas import tpu as pltpu
from jax.sharding import PartitionSpec as P

EXPERTS = 32
MOST = 26
BF16 = jnp.bfloat16
F32 = jnp.float32
MIB = 1 << 20

NN = (((1,), (0,)), ((), ()))
NT = (((1,), (1,)), ((), ()))
TN = (((0,), (0,)), ((), ()))


def dot(a, b, dims=NN):
    return lax.dot_general(a, b, dims, preferred_element_type=F32)


def rotate(block, axis, distance):
    n = lax.axis_size(axis)
    return lax.ppermute(block, axis, [(i, (i + distance) % n) for i in range(n)])


def swap(block, axis, mask):
    n = lax.axis_size(axis)
    return lax.ppermute(block, axis, [(i, i ^ mask) for i in range(n)])


def after(value, *others):
    return lax.optimization_barrier((value, *others))[0]


def params(slots):
    return pltpu.CompilerParams(vmem_limit_bytes=(40 if slots <= 128 else 48) * MIB)


def cost(flops, nbytes):
    return pl.CostEstimate(flops=int(flops), bytes_accessed=int(nbytes), transcendentals=0)


def routing_kernel(slots, dest_ref, weight_ref, dest_col_ref, weight_col_ref, *refs):
    ordered_refs, mix_refs, slot_weight_ref = refs[:2], refs[2:4], refs[4]
    total, tokens = ordered_refs[0].shape
    local = total // slots
    place = lax.broadcasted_iota(jnp.int32, (slots, tokens), 0)
    slot = lax.broadcasted_iota(jnp.int32, (tokens, total), 1)
    for way in range(2):
        mix = jnp.zeros((tokens, total), F32)
        for l in range(local):
            at = way * local + l
            part = slice(l * slots, (l + 1) * slots)
            hit = place == dest_ref[at : at + 1, :]
            ordered_refs[way][part, :] = jnp.where(hit, 1.0, 0.0).astype(BF16)
            if way == 1:
                slot_weight_ref[part, :] = jnp.sum(
                    jnp.where(hit, weight_ref[at : at + 1, :], 0.0), 1, keepdims=True
                )
            here = dest_col_ref[:, at : at + 1]
            here = jnp.where(here >= 0, here + l * slots, -1)
            value = weight_col_ref[:, at : at + 1] if way == 0 else 1.0
            mix = jnp.where(slot == here, value, mix)
        mix_refs[way][...] = mix.astype(BF16)


def routing_matrices(dest, weight, slots):
    tokens, both = dest.shape
    total = both // 2 * slots
    return pl.pallas_call(
        functools.partial(routing_kernel, slots),
        out_shape=[jax.ShapeDtypeStruct((total, tokens), BF16)] * 2
        + [jax.ShapeDtypeStruct((tokens, total), BF16)] * 2
        + [jax.ShapeDtypeStruct((total, 1), F32)],
        compiler_params=params(slots),
        cost_estimate=cost(0, 8 * total * tokens),
        name="routing",
    )(dest.T, weight.T, dest, weight)


def order_kernel(n_pieces, onehot_ref, *refs):
    *pieces, out_ref, rows_ref = refs
    at = 0
    for piece in pieces:
        rows_ref[at : at + piece.shape[0], :] = piece[...]
        at += piece.shape[0]
    out_ref[...] = dot(onehot_ref[...], rows_ref[...]).astype(BF16)


def weighted_order_kernel(n_pieces, plain, onehot_ref, slot_weight_ref, *refs):
    *pieces, out_ref, rows_ref = refs
    at = 0
    for piece in pieces:
        rows_ref[at : at + piece.shape[0], :] = piece[...]
        at += piece.shape[0]
    ordered = dot(onehot_ref[...], rows_ref[...])
    scale = jnp.where(pl.program_id(0) < plain, 1.0, slot_weight_ref[...])
    out_ref[...] = (ordered * scale).astype(BF16)


def in_expert_order(onehot, pieces, slot_weight=None):
    total, tokens = onehot.shape
    width = pieces[0].shape[1]
    chunk = min(2048 if tokens <= 512 else 512, width)
    steps = width // chunk
    in_specs = [pl.BlockSpec((total, tokens), lambda c: (0, 0))]
    operands = [onehot]
    if slot_weight is None:
        kernel = functools.partial(order_kernel, len(pieces))
    else:
        kernel = functools.partial(weighted_order_kernel, len(pieces), steps // 2)
        in_specs.append(pl.BlockSpec((total, 1), lambda c: (0, 0)))
        operands.append(slot_weight)
    in_specs += [pl.BlockSpec((piece.shape[0], chunk), lambda c: (0, c)) for piece in pieces]
    return pl.pallas_call(
        kernel,
        grid=(steps,),
        in_specs=in_specs,
        out_specs=pl.BlockSpec((total, chunk), lambda c: (0, c)),
        out_shape=jax.ShapeDtypeStruct((total, width), BF16),
        scratch_shapes=[pltpu.VMEM((tokens, chunk), BF16)],
        compiler_params=params(total // 8),
        cost_estimate=cost(2 * total * tokens * width, 2 * (total + tokens) * width),
        name="order_rows",
    )(*operands, *pieces)


def combine_kernel(mix_ref, rows_ref, keep_ref, send_ref):
    half = mix_ref.shape[0] // 2
    summed = dot(mix_ref[...], rows_ref[...]).astype(BF16)
    keep_ref[...] = summed[:half]
    send_ref[...] = summed[half:]


def token_sums(mix, rows, part, parts):
    tokens, total = mix.shape
    width = rows.shape[1] // parts
    chunk = min(2048 if tokens <= 512 else 512, width)
    steps = width // chunk
    return pl.pallas_call(
        combine_kernel,
        grid=(steps,),
        in_specs=[
            pl.BlockSpec((tokens, total), lambda c: (0, 0)),
            pl.BlockSpec((total, chunk), lambda c: (0, c + part * steps)),
        ],
        out_specs=[pl.BlockSpec((tokens // 2, chunk), lambda c: (0, c))] * 2,
        out_shape=[jax.ShapeDtypeStruct((tokens // 2, width), BF16)] * 2,
        compiler_params=params(total // 8),
        cost_estimate=cost(2 * total * tokens * width, 2 * (total + tokens) * width),
        name="token_sums",
    )(mix, rows)


def forward_kernel(rows_ref, gate_ref, up_ref, down_ref, out_ref):
    rows = rows_ref[...]
    gate_value = dot(rows, gate_ref[0])
    up_value = dot(rows, up_ref[0])
    hidden = (gate_value / (1.0 + jnp.exp(-gate_value)) * up_value).astype(BF16)
    out_ref[...] = dot(hidden, down_ref[0]).astype(BF16)


def backward_kernel(
    rows_ref, grad_ref, gate_ref, up_ref, down_ref, hidden_ref, gate_grad_ref, up_grad_ref, out_ref
):
    rows = rows_ref[...]
    gate_value = dot(rows, gate_ref[0])
    up_value = dot(rows, up_ref[0])
    hidden_grad = dot(grad_ref[...], down_ref[0], NT)
    sig = 1.0 / (1.0 + jnp.exp(-gate_value))
    silu = gate_value * sig
    hidden_ref[...] = (silu * up_value).astype(BF16)
    up_grad = (hidden_grad * silu).astype(BF16)
    gate_grad = (hidden_grad * up_value * sig * (1.0 + gate_value * (1.0 - sig))).astype(BF16)
    up_grad_ref[...] = up_grad
    gate_grad_ref[...] = gate_grad
    width = out_ref.shape[1]
    for at in range(0, width, 512):
        part = slice(at, min(at + 512, width))
        row_grad = dot(gate_grad, gate_ref[0, part], NT) + dot(up_grad, up_ref[0, part], NT)
        out_ref[:, part] = row_grad.astype(BF16)


def weights_kernel(
    rows_ref, grad_ref, hidden_ref, gate_grad_ref, up_grad_ref, gate_ref, up_ref, down_ref
):
    rows = rows_ref[...]
    gate_ref[0] = dot(rows, gate_grad_ref[...], TN).astype(BF16)
    up_ref[0] = dot(rows, up_grad_ref[...], TN).astype(BF16)
    down_ref[0] = dot(hidden_ref[...], grad_ref[...], TN).astype(BF16)


def expert_specs(local, slots, width, hidden):
    wide = pl.BlockSpec((slots, width), lambda e: (e, 0))
    narrow = pl.BlockSpec((slots, hidden), lambda e: (e, 0))
    column = pl.BlockSpec((1, width, hidden), lambda e: (e, 0, 0))
    row = pl.BlockSpec((1, hidden, width), lambda e: (e, 0, 0))
    return wide, narrow, column, row


def forward_experts(rows, gate, up, down):
    local, width, hidden = gate.shape
    slots = rows.shape[0] // local
    wide, narrow, column, row = expert_specs(local, slots, width, hidden)
    return pl.pallas_call(
        forward_kernel,
        grid=(local,),
        in_specs=[wide, column, column, row],
        out_specs=wide,
        out_shape=jax.ShapeDtypeStruct(rows.shape, BF16),
        compiler_params=params(slots),
        cost_estimate=cost(6 * rows.shape[0] * width * hidden, 6 * local * width * hidden),
        name="forward_experts",
    )(rows, gate, up, down)


def backward_experts(both, gate, up, down):
    local, width, hidden = gate.shape
    total = both.shape[0]
    slots = total // local
    wide, narrow, column, row = expert_specs(local, slots, width, hidden)
    grad_wide = pl.BlockSpec((slots, width), lambda e: (e, 1))
    small = jax.ShapeDtypeStruct((total, hidden), BF16)
    return pl.pallas_call(
        backward_kernel,
        grid=(local,),
        in_specs=[wide, grad_wide, column, column, row],
        out_specs=[narrow, narrow, narrow, wide],
        out_shape=[small, small, small, jax.ShapeDtypeStruct((total, width), BF16)],
        compiler_params=params(slots),
        cost_estimate=cost(10 * total * width * hidden, 6 * local * width * hidden),
        name="backward_experts",
    )(both, both, gate, up, down)


def weight_grads(both, hidden_rows, gate_grad, up_grad, local):
    total, hidden = gate_grad.shape
    width = both.shape[1] // 2
    slots = total // local
    grad_wide = pl.BlockSpec((slots, width), lambda e: (e, 1))
    wide, narrow, column, row = expert_specs(local, slots, width, hidden)
    return pl.pallas_call(
        weights_kernel,
        grid=(local,),
        in_specs=[wide, grad_wide, narrow, narrow, narrow],
        out_specs=[column, column, row],
        out_shape=[
            jax.ShapeDtypeStruct((local, width, hidden), BF16),
            jax.ShapeDtypeStruct((local, width, hidden), BF16),
            jax.ShapeDtypeStruct((local, hidden, width), BF16),
        ],
        compiler_params=params(slots),
        cost_estimate=cost(6 * total * width * hidden, 6 * local * width * hidden),
        name="weight_grads",
    )(both, both, hidden_rows, gate_grad, up_grad)


def halves(block, dp_index):
    half = block.shape[0] // 2
    mine = lax.dynamic_slice_in_dim(block, dp_index * half, half, 0)
    other = lax.dynamic_slice_in_dim(block, (1 - dp_index) * half, half, 0)
    return mine, other


def cross(block, axis, mask):
    n, m = lax.axis_size(axis), lax.axis_size("dp")
    route = [(i * m + d, (i ^ mask) * m + (m - 1 - d)) for i in range(n) for d in range(m)]
    return lax.ppermute(block, (axis, "dp"), route)


def spread_meta(meta, dp_index, groups):
    half = meta.shape[0] // 2
    both = jnp.concatenate(halves(meta, dp_index), 0)
    if groups != 4:
        metas = list(lax.all_gather(both, "expert"))
    else:
        metas = [both] + [swap(both, "expert", r) for r in range(1, groups)]
    return jnp.concatenate([m[:half] for m in metas] + [m[half:] for m in metas], 0)


def sums_sent(keep, received, groups):
    pair = (keep.astype(F32) + received.astype(F32)).astype(BF16)
    pair = pair.reshape(groups, keep.shape[0] // groups, -1)
    if groups != 4:
        return [lax.all_to_all(pair, "expert", 0, 0, tiled=True)]
    return [pair[0]] + [swap(pair[r], "expert", r) for r in range(groups - 1, 0, -1)]


def sums_home(base, sent):
    total = base.astype(F32)
    for piece in sent:
        piece = piece.astype(F32)
        total = total + (jnp.sum(piece, 0) if piece.ndim == 3 else piece)
    return total.astype(BF16)


def to_section(mine, direction, dp_index):
    n, m = lax.axis_size("section"), lax.axis_size("dp")
    same = rotate(mine, "section", direction)
    route = [
        (s * m + d, ((s + direction) % n) * m + (m - 1 - d)) for s in range(n) for d in range(m)
    ]
    other = lax.ppermute(mine, ("section", "dp"), route)
    first = jnp.where(dp_index == 0, same, other)
    second = jnp.where(dp_index == 0, other, same)
    return jnp.concatenate([first, second], 0)


def slot_tables(meta, choices, base, local):
    tokens = meta.shape[0]
    meta = meta.reshape(tokens, 2, 2, choices)
    routes, counted = meta[:, :, 0], meta[:, :, 1].astype(F32)
    mixing = counted / jnp.sum(counted, -1, keepdims=True)
    hit = (routes[..., None] - base) == jnp.arange(local, dtype=jnp.int32)
    weight = jnp.sum(jnp.where(hit, mixing[..., None], 0.0), 2)
    chosen = jnp.any(hit, 2).astype(jnp.int32)
    rank = jnp.cumsum(chosen, 0) - chosen
    dest = jnp.where(chosen > 0, rank, -1)
    return dest.reshape(tokens, -1), weight.reshape(tokens, -1)


def local(
    fwd_in, fwd_routes, fwd_numer, bwd_saved, bwd_routes, bwd_numer, bwd_grad, w_gate, w_up, w_down
):
    groups = lax.axis_size("expert")
    group, dp_index = lax.axis_index("expert"), lax.axis_index("dp")
    gate, up, down = w_gate[0], w_up[0], w_down[0]
    n_local = gate.shape[0]
    choices = fwd_routes.shape[-1]
    slots = -(-groups * MOST // 16) * 16

    meta = jnp.concatenate([fwd_routes[0], fwd_numer[0], bwd_routes[0], bwd_numer[0]], -1)
    in_mine, in_other = halves(fwd_in[0], dp_index)
    back_mine, back_other = halves(jnp.concatenate([bwd_saved[0], bwd_grad[0]], 1), dp_index)
    meta_all = spread_meta(after(meta, back_mine), dp_index, groups)
    dest, weight = slot_tables(meta_all, choices, group * n_local, n_local)
    grad_mine, _ = halves(bwd_grad[0], dp_index)

    if groups == 4:
        near, past = swap(in_mine, "expert", 1), swap(after(in_mine, back_mine), "expert", 2)
        back_near = swap(after(back_mine, near, past), "expert", 1)
        last = swap(past, "expert", 1)
        far = [swap(near, "dp", 1), swap(past, "dp", 1), swap(last, "dp", 1)]
        back_past = swap(after(back_mine, last), "expert", 2)
        in_pieces = [in_mine, near, past, last, in_other, *far]
    else:
        near = lax.all_gather(in_mine, "expert", tiled=True)
        back_near = lax.all_gather(back_mine, "expert", tiled=True)
        back_past = ()
        in_pieces = [near, swap(near, "dp", 1)]

    ordered, back_ordered, mix, back_mix, slot_weight = routing_matrices(dest, weight, slots)
    ordered, back_near = lax.optimization_barrier((ordered, back_near))
    back_far = swap(back_near, "dp", 1)
    in_rows = in_expert_order(ordered, in_pieces)
    in_rows, back_past = lax.optimization_barrier((in_rows, back_past))
    if groups == 4:
        back_last = swap(back_past, "expert", 1)
        back_far = [back_far, swap(back_past, "dp", 1), cross(back_past, "expert", 1)]
        back_pieces = [back_mine, back_near, back_past, back_last, back_other, *back_far]
    else:
        back_pieces = [back_near, back_far]
    out_rows = forward_experts(in_rows, gate, up, down)
    out_keep, out_send = token_sums(mix, out_rows, 0, 1)
    out_received = swap(after(out_send, back_pieces[-1]), "dp", 1)

    back_rows = in_expert_order(back_ordered, back_pieces, slot_weight)
    hidden, gate_grad, up_grad, row_grad = backward_experts(back_rows, gate, up, down)
    row_grad, out_received = lax.optimization_barrier((row_grad, out_received))
    out_sent = sums_sent(out_keep, out_received, groups)
    keep, send = token_sums(back_mix, row_grad, 0, 1)
    received = swap(send, "dp", 1)
    gate_grad = after(gate_grad, keep)
    gate_sum, up_sum, down_sum = weight_grads(back_rows, hidden, gate_grad, up_grad, n_local)
    gate_sum, received, *out_sent = lax.optimization_barrier((gate_sum, received, *out_sent))
    sent = sums_sent(keep, received, groups)
    next_fwd = to_section(sums_home(in_mine, out_sent), 1, dp_index)
    next_bwd = to_section(sums_home(grad_mine, sent), -1, dp_index)
    return (next_fwd[None], next_bwd[None], gate_sum[None], up_sum[None], down_sum[None])


def solution(mesh):
    in_specs = (
        P("section", "expert", None),
        P("section", "expert", None),
        P("section", "expert", None),
        P("section", "expert", None),
        P("section", "expert", None),
        P("section", "expert", None),
        P("section", "expert", None),
        P("section", "expert", None, "dp"),
        P("section", "expert", None, "dp"),
        P("section", "expert", "dp", None),
    )
    out_specs = (
        P("section", "expert", None),
        P("section", "expert", None),
        P("section", "expert", None, "dp"),
        P("section", "expert", None, "dp"),
        P("section", "expert", "dp", None),
    )
    return jax.shard_map(local, mesh=mesh, in_specs=in_specs, out_specs=out_specs, check_vma=False)
```
